512 devices in a mesh: patch: 32 (over x_hi, z, core), freq: 16 (over y, x_lo).
Axes of the slice: x: 4 (x_hi: 2, x_lo: 2; x = x_hi * 2 + x_lo), y: 8, z: 8, core: 2. Of those that a mesh axis runs over, the one named last changes fastest.
Arguments:
- slip_rate: bfloat16 [2688, 4096], P('patch', 'freq'), may hold values from -6 to 6
- face_counts: int32 [32], P('patch'), may hold values from 12 to 84, as said below
- patch_ids: int32 [2688], P('patch'), may hold values from 0 to 1535, as said below
- moments: float32 [1536, 6], P('patch'), may hold values from -6 to 6
- green: bfloat16 [6, 2, 3, 496, 49152], P(None, None, None, 'freq', 'patch'), may hold values from -0.046875 to 0.046875
Outputs:
- seismograms: float32 [3, 496, 4096], P(None, 'freq', 'patch')
The draws below stay inside these ranges and needn't reach their ends.
Inputs may be any that keep to these rules, and one draw needn't show every extreme that they name: The live slots of face i are its first face_counts[i] slots; the counts sum to 1536, one face has all 84 slots live and one has only 12. `patch_ids`: over the live slots of all faces every patch number appears exactly once; a dead slot holds an arbitrary patch number.
All inputs are finite; a program needn't handle non-finite values.
Results may differ from the reference program's by a relative error of at most 0.0029.
Values may be sent and summed in bfloat16 or wider, within the bound.
No kernel may reach another device: no remote copies, remote signals or barrier semaphores. Data moves between devices by JAX's collectives and lax.ppermute only.
A program may use at most 128 MiB of HBM per device.

```python
import math
import jax
import jax.numpy as jnp
from jax import lax

TIME_STEP_TOTAL = 4096
SPECTRAL_LINES = 32
STA = 496
P_DEV = 48
HALF = 36
CAP = 84
PATCHES = 1536
SLOTS = 2688
N_PATCH = 32


def faces_layout(key):
    order_key, rise_key, spot_key, perm_key, junk_key = jax.random.split(key, 5)
    order = jax.random.permutation(order_key, N_PATCH)
    rises = jax.random.randint(rise_key, (N_PATCH,), 0, HALF + 1)
    spot = jax.random.randint(spot_key, (), 0, N_PATCH)
    places = jnp.arange(N_PATCH, dtype=jnp.int32)
    rises = jnp.where(places == spot, HALF, rises)
    rises = jnp.where(places == (spot + 1) % N_PATCH, 0, rises)
    rises = jnp.where(places == (spot + N_PATCH - 1) % N_PATCH, 0, rises)
    sequence = (P_DEV + rises - jnp.roll(rises, -1)).astype(jnp.int32)
    counts = jnp.zeros((N_PATCH,), jnp.int32).at[order].set(sequence)
    offsets = jnp.cumsum(counts) - counts
    shuffled = jax.random.permutation(perm_key, PATCHES).astype(jnp.int32)
    column = jnp.arange(CAP, dtype=jnp.int32)[None, :]
    position = jnp.clip(offsets[:, None] + column, 0, PATCHES - 1)
    junk = jax.random.randint(junk_key, (N_PATCH, CAP), 0, PATCHES).astype(jnp.int32)
    numbers = jnp.where(column < counts[:, None], shuffled[position], junk)
    return (counts, numbers.reshape(N_PATCH * CAP))


def draw_face_counts(key, part):
    return faces_layout(key)[0]


def draw_patch_ids(key, part):
    return faces_layout(key)[1]


def level_of(rng, shape, shards, least, top_value):
    factor_of, own = 1.0, jax.random.fold_in(rng, 6)
    for dim, shards_of in shards:
        heights = jnp.exp(jax.random.uniform(jax.random.fold_in(own, dim), (shards_of,), jnp.float32, least / len(shards), top_value / len(shards)))
        factor_of = factor_of * jnp.repeat(heights, shape[dim] // shards_of).reshape([-1 if axis == dim else 1 for axis in range(len(shape))])
    return factor_of


def noise(own_key, extent, deviation, reach, shards=(), kind=jnp.bfloat16):
    drawn = deviation * jax.random.normal(own_key, extent, jnp.float32)
    if shards:
        drawn = drawn * level_of(own_key, extent, shards, -0.22, 0.18)
    return jnp.clip(drawn, -reach, reach).astype(kind)


def setup_inputs(seed: int = 0) -> dict:
    streams_of = jax.random.split(jax.random.key(seed), 6)
    slip_rate = noise(streams_of[0], (SLOTS, TIME_STEP_TOTAL), 1.0, 6.0, ((0, 32), (1, 16)))
    face_counts = draw_face_counts(jax.random.fold_in(streams_of[5], 71), 0)
    patch_ids = draw_patch_ids(jax.random.fold_in(streams_of[5], 71), 0)
    moments = noise(streams_of[3], (PATCHES, 6), 1.0, 6.0, ((0, 32),), jnp.float32)
    green = noise(streams_of[4], (6, 2, 3, STA, PATCHES * SPECTRAL_LINES), (12 * PATCHES) ** -0.5, 0.046875, ((3, 16), (4, 32)))
    return {"slip_rate": slip_rate, "face_counts": face_counts, "patch_ids": patch_ids, "moments": moments, "green": green}


def mode_indices():
    return 1 + jnp.arange(SPECTRAL_LINES, dtype=jnp.int32) * (TIME_STEP_TOTAL // (2 * SPECTRAL_LINES))

def analysis_kernel(discrete_epochs):
    oscillation_argument = (discrete_epochs[:, None] * mode_indices()[None, :] % TIME_STEP_TOTAL).astype(jnp.float32) * (2.0 * math.pi / TIME_STEP_TOTAL)
    layered_recordings = jnp.stack([jnp.cos(oscillation_argument), -jnp.sin(oscillation_argument)], axis=-1) * (1.0 / math.sqrt(TIME_STEP_TOTAL))
    return layered_recordings.reshape(discrete_epochs.shape[0], 2 * SPECTRAL_LINES)

def synthesis_kernel(discrete_epochs):
    oscillation_argument = (mode_indices()[:, None] * discrete_epochs[None, :] % TIME_STEP_TOTAL).astype(jnp.float32) * (2.0 * math.pi / TIME_STEP_TOTAL)
    layered_recordings = jnp.stack([jnp.cos(oscillation_argument), -jnp.sin(oscillation_argument)], axis=1) * (1.0 / math.sqrt(SPECTRAL_LINES))
    return layered_recordings.reshape(2 * SPECTRAL_LINES, discrete_epochs.shape[0])

def mixing(spectrum, moments):
    real_part = spectrum[:, :, 0]
    imag_part = spectrum[:, :, 1]
    along_real = moments[:, :, None] * real_part[:, None, :]
    along_imag = moments[:, :, None] * imag_part[:, None, :]
    upper = jnp.stack([along_real, -along_imag])
    lower = jnp.stack([along_imag, along_real])
    return jnp.stack([upper, lower]).astype(jnp.bfloat16)

def reference(slip_rate, face_counts, patch_ids, moments, green):
    slot_total = slip_rate.shape[0]
    capacity = slot_total // N_PATCH
    alive_mask = (jnp.arange(capacity, dtype=jnp.int32)[None, :] < face_counts[:, None]).reshape(slot_total)
    recorded_waveform = jnp.where(alive_mask[:, None], slip_rate.astype(jnp.float32), 0.0)
    slot_spectra = jnp.dot(recorded_waveform, analysis_kernel(jnp.arange(TIME_STEP_TOTAL, dtype=jnp.int32)), precision=lax.Precision.HIGHEST)
    target = jnp.where(alive_mask, patch_ids, PATCHES)
    spectra = jnp.zeros((PATCHES, 2 * SPECTRAL_LINES), jnp.float32).at[target].add(slot_spectra, mode='drop')
    weights = mixing(spectra.reshape(PATCHES, SPECTRAL_LINES, 2), moments)
    tiles = green.reshape(6, 2, 3, STA, PATCHES, SPECTRAL_LINES)

    def one_bin(bin_index):
        frequency_weight = lax.dynamic_index_in_dim(weights, bin_index, 4, keepdims=False).astype(jnp.float32)
        frequency_tile = lax.dynamic_index_in_dim(tiles, bin_index, 5, keepdims=False).astype(jnp.float32)
        return jnp.einsum('xeir,requi->xqu', frequency_weight, frequency_tile, precision=lax.Precision.HIGHEST)
    totals = lax.map(one_bin, jnp.arange(SPECTRAL_LINES, dtype=jnp.int32))
    unrolled_records = totals.reshape(2 * SPECTRAL_LINES, 3 * STA)
    seismograms = jnp.dot(unrolled_records.T, synthesis_kernel(jnp.arange(TIME_STEP_TOTAL, dtype=jnp.int32)), precision=lax.Precision.HIGHEST)
    return seismograms.reshape(3, STA, TIME_STEP_TOTAL)
```

```python
import functools
import math

import jax
import jax.numpy as jnp
import numpy as np
from jax import lax
from jax.experimental import pallas as pl
from jax.experimental.pallas import tpu as pltpu
from jax.sharding import PartitionSpec as P

T = 4096
BINS = 32
FACES = 32
WINDOWS = 16
CAP = 84
OWN = 48
STA_DEV = 31
HOLD = 96
ID_ROW = 88

CORE_PAIRS = [[2 * d, 2 * d + 1] for d in range(16)]
SAME_CORE = [[2 * d + c for d in range(16)] for c in range(2)]

f32 = jnp.float32
bf16 = jnp.bfloat16


def split2(x):
    hi = x.astype(bf16)
    return hi, (x - hi.astype(f32)).astype(bf16)


def np_split2(x):
    hi = x.astype(np.float32).astype(jnp.bfloat16)
    lo = (x - hi.astype(np.float64)).astype(np.float32).astype(jnp.bfloat16)
    return hi, lo


def angles(samples):
    k = 1 + np.arange(BINS) * (T // (2 * BINS))
    return 2.0 * np.pi * ((np.arange(samples)[:, None] * k[None, :]) % T) / T


def analysis_table():
    ang = angles(T // WINDOWS)
    c, s = np.cos(ang) / math.sqrt(T), np.sin(ang) / math.sqrt(T)
    straight = np.concatenate([c, -s, c, -s], axis=1)
    turned = np.concatenate([-s, -c, -s, -c], axis=1)
    s_hi, s_lo = np_split2(straight)
    t_hi, t_lo = np_split2(turned)
    return np.concatenate([s_hi, t_hi, s_lo, t_lo], axis=1)


def synthesis_table():
    ang = angles(T // FACES).T
    c, s = np.cos(ang) / math.sqrt(BINS), -np.sin(ang) / math.sqrt(BINS)
    z = np.zeros_like(c)
    first = np.concatenate([c, z, s, z], axis=0)
    second = np.concatenate([z, c, z, s], axis=0)
    hi, lo = np_split2(np.concatenate([first, second], axis=1))
    return np.concatenate([hi, hi, lo], axis=0)


def turns(n):
    a = 2.0 * np.pi * np.arange(n) / n
    return np.concatenate([np.cos(a), np.sin(a)]).astype(np.float32)


def lanes(shape):
    return lax.broadcasted_iota(jnp.int32, shape, len(shape) - 1)


def rows(shape):
    return lax.broadcasted_iota(jnp.int32, shape, len(shape) - 2)


def window_kernel(count, turn, slip, ids, table, out):
    q = lax.axis_index("freq")
    r = jnp.dot(slip[...], table[...], preferred_element_type=f32)
    x = turn[q] * (r[:, :128] + r[:, 256:384]) + turn[q + WINDOWS] * (
        r[:, 128:256] + r[:, 384:]
    )
    out[0:CAP, :] = jnp.where(rows((CAP, 128)) < count[0], x, 0.0)
    out[ID_ROW:HOLD, :] = jnp.full((HOLD - ID_ROW, 128), -1.0, f32)
    out[CAP:ID_ROW, :] = jnp.zeros((ID_ROW - CAP, 128), f32)
    live = lanes((1, CAP)) < count[0]
    out[ID_ROW : ID_ROW + 1, 0:CAP] = jnp.where(live, ids[...].astype(f32), -1.0)


def route_kernel(held, out):
    core = lax.rem(lax.axis_index("patch"), 2).astype(f32)
    n = 16 * 24
    r = rows((n, 128))
    d = lax.shift_right_logical(r * 2731, 16)
    j = lax.shift_right_logical(r - 24 * d, 1)
    base = (96 * d + 4 * j).astype(f32)
    block = lax.shift_right_logical(lanes((HOLD, 256)), 5) % 4
    odd = lax.rem(lax.shift_right_logical(lanes((HOLD, 128)), 5), 2) == 1
    left, right_hi, right_lo = [], [], []
    for k in range(2):
        x = held[k]
        re = jnp.where(odd, pltpu.roll(x, 32, 1), x)
        im = jnp.where(odd, x, pltpu.roll(x, 96, 1))
        hi, lo = split2(jnp.concatenate([re, im], axis=1))
        hi, lo = hi.astype(f32), lo.astype(f32)
        owner = held[k, ID_ROW : ID_ROW + 1, :]
        ahead = owner - base - 48.0 * core
        pad = jnp.zeros((128 - HOLD, 256), f32)
        for b in range(4):
            left.append(jnp.where(ahead == float(b), 1.0, 0.0))
            right_hi.append(jnp.where(block == b, hi, 0.0))
            right_hi.append(pad)
            right_lo.append(jnp.where(block == b, lo, 0.0))
            right_lo.append(pad)
    lhs = jnp.concatenate(left, axis=1).astype(bf16)
    rhs_hi = jnp.concatenate(right_hi, axis=0).astype(bf16)
    rhs_lo = jnp.concatenate(right_lo, axis=0).astype(bf16)
    got = jnp.dot(lhs, rhs_hi, preferred_element_type=f32) + jnp.dot(
        lhs, rhs_lo, preferred_element_type=f32
    )
    even = lax.rem(r, 2) == 0
    out[...] = jnp.where(even, got[:, :128], got[:, 128:]).reshape(16, 24, 128)


def spread_kernel(got, out):
    total = jnp.sum(got[...], axis=0)
    out[...] = jnp.broadcast_to(total[None], out.shape)


def sublane_sums(parts):
    sub = rows((8, 128))
    dist = 4
    while dist >= 1:
        low = (lax.shift_right_logical(sub, dist.bit_length() - 1) % 2) == 0
        parts = [
            jnp.where(low, a, b) + pltpu.roll(jnp.where(low, b, a), dist, 0)
            if dist == 4
            else jnp.where(low, a, b)
            + jnp.where(
                low, pltpu.roll(a, 8 - dist, 0), pltpu.roll(b, dist, 0)
            )
            for a, b in zip(parts[: len(parts) // 2], parts[len(parts) // 2 :])
        ]
        dist //= 2
    return parts[0]


def green_kernel(green, moments, got, out):
    s = jnp.sum(got[...], axis=0)
    even = lax.rem(rows((24, 128)), 2) == 0
    swapped = jnp.where(even, pltpu.roll(s, 23, 0), pltpu.roll(s, 1, 0))
    for_re = jnp.where(even, s, -s)
    for_im = swapped
    pick = lax.shift_right_logical(rows((24, OWN)), 1) == lax.shift_right_logical(
        lanes((24, OWN)), 2
    )
    spread = jnp.where(
        lax.rem(rows((OWN, 128)), 4) == lax.shift_right_logical(lanes((OWN, 128)), 5),
        1.0,
        0.0,
    ).astype(bf16)
    m_rows = jnp.concatenate(
        [jnp.where(pick, moments[m : m + 1, :], 0.0) for m in range(6)], axis=0
    )
    m_hi, m_lo = split2(m_rows)
    m_all = jnp.dot(m_hi, spread, preferred_element_type=f32) + jnp.dot(
        m_lo, spread, preferred_element_type=f32
    )
    lane = lanes((8, 128))
    half = lane < 64
    block_even = lax.rem(lax.shift_right_logical(lane, 5), 2) == 0
    stride = 3 * STA_DEV * 24
    folded = []
    for c in range(3):
        for s0 in range(0, 32, 8):
            n = min(8, STA_DEV - s0)
            acc = None
            for m in range(6):
                start = m * stride + (c * STA_DEV + s0) * 24
                stop = start + n * 24
                a, z = start // 16 * 16, -(-stop // 16) * 16
                g = green[a:z, :].astype(f32)[start - a : stop - a]
                w = m_all[24 * m : 24 * m + 24]
                term = g.reshape(n, 24, 128) * w[None]
                acc = term if acc is None else acc + term
            sums = []
            for weight in (for_re, for_im):
                p = (acc * weight[None]).reshape(n, 3, 8, 128)
                p = p[:, 0] + p[:, 1] + p[:, 2]
                parts = [p[i] for i in range(n)] + [jnp.zeros((8, 128), f32)] * (8 - n)
                sums.append(sublane_sums(parts))
            a, b = sums
            folded.append(
                jnp.where(half, a, b) + pltpu.roll(jnp.where(half, b, a), 64, 1)
            )
    for i in range(6):
        a, b = folded[i], folded[i + 6]
        w = jnp.where(block_even, a, b)
        z = jnp.where(block_even, pltpu.roll(a, 96, 1), pltpu.roll(b, 32, 1))
        out[8 * i : 8 * i + 8, :] = w + z


def series_kernel(turn, got, table, out):
    p = lax.axis_index("patch")
    x = jnp.sum(got[...], axis=0)
    other = pltpu.roll(x, 64, 1)
    real = lanes((48, 128)) < 64
    x = turn[p] * x + turn[p + FACES] * jnp.where(real, -other, other)
    hi, lo = split2(x)
    lhs = jnp.concatenate([hi, lo, hi], axis=1)
    y = jnp.dot(lhs, table[...], preferred_element_type=f32)
    y = jnp.concatenate([y[:, :128], y[:, 128:]], axis=0)
    for c in range(3):
        out[c] = y[32 * c : 32 * c + STA_DEV]


VMEM = pl.BlockSpec(memory_space=pltpu.VMEM)
SMEM = pl.BlockSpec(memory_space=pltpu.SMEM)


def call(kernel, shape, specs, *args, dtype=f32):
    return pl.pallas_call(
        kernel,
        out_shape=jax.ShapeDtypeStruct(shape, dtype),
        in_specs=specs,
        out_specs=VMEM,
        compiler_params=pltpu.CompilerParams(vmem_limit_bytes=32 * 1024 * 1024),
    )(*args)


def local(slip_rate, face_counts, patch_ids, moments, green):
    held = call(
        window_kernel,
        (HOLD, 128),
        [SMEM, SMEM, VMEM, VMEM, VMEM],
        face_counts,
        jnp.asarray(turns(WINDOWS)),
        slip_rate,
        patch_ids.reshape(1, CAP),
        jnp.asarray(analysis_table()),
    )
    held = lax.all_gather(held, "patch", axis_index_groups=CORE_PAIRS)
    blocks = call(route_kernel, (16, 24, 128), [VMEM], held)
    blocks = lax.all_to_all(
        blocks, "patch", 0, 0, axis_index_groups=SAME_CORE, tiled=True
    )
    copies = call(spread_kernel, (16, 24, 128), [VMEM], blocks)
    copies = lax.all_to_all(copies, "freq", 0, 0, tiled=True)
    tiles = green.transpose(0, 2, 3, 1, 4).reshape(6, 3, STA_DEV, 2, 12, 128)
    tiles = tiles.transpose(0, 1, 2, 4, 3, 5).reshape(6 * 3 * STA_DEV * 24, 128)
    partial = call(
        green_kernel, (48, 128), [VMEM, VMEM, VMEM], tiles, moments.T, copies
    )
    pair = lax.all_gather(partial, "patch", axis_index_groups=CORE_PAIRS)
    copies = call(spread_kernel, (16, 48, 128), [VMEM], pair)
    copies = lax.all_to_all(
        copies, "patch", 0, 0, axis_index_groups=SAME_CORE, tiled=True
    )
    return call(
        series_kernel,
        (3, STA_DEV, 128),
        [SMEM, VMEM, VMEM],
        jnp.asarray(turns(FACES)),
        copies,
        jnp.asarray(synthesis_table()),
    )


def solution(mesh):
    return jax.shard_map(
        local,
        mesh=mesh,
        in_specs=(
            P("patch", "freq"),
            P("patch"),
            P("patch"),
            P("patch", None),
            P(None, None, None, "freq", "patch"),
        ),
        out_specs=P(None, "freq", "patch"),
        check_vma=False,
    )
```

```python
import functools
import math

import jax
import jax.numpy as jnp
import numpy as np
from jax import lax
from jax.experimental import pallas as pl
from jax.experimental.pallas import tpu as pltpu
from jax.sharding import PartitionSpec as P

T = 4096
BINS = 32
FACES = 32
WINDOWS = 16
CAP = 84
OWN = 48
STA_DEV = 31
HOLD = 96
ID_ROW = 88

CORE_PAIRS = [[2 * d, 2 * d + 1] for d in range(16)]
SAME_CORE = [[2 * d + c for d in range(16)] for c in range(2)]

f32 = jnp.float32
bf16 = jnp.bfloat16


def split2(x):
    hi = x.astype(bf16)
    return hi, (x - hi.astype(f32)).astype(bf16)


def angles(samples):
    k = 1 + np.arange(BINS) * (T // (2 * BINS))
    return 2.0 * np.pi * ((np.arange(samples)[:, None] * k[None, :]) % T) / T


def analysis_table():
    t = np.arange(T)[:, None]
    k = 1 + np.arange(BINS) * (T // (2 * BINS))
    ang = 2.0 * np.pi * ((t * k) % T) / T
    c, s = np.cos(ang) / math.sqrt(T), -np.sin(ang) / math.sqrt(T)
    table = np.concatenate([c, s, c, s], axis=1).astype(np.float32)
    return table.reshape(WINDOWS, T // WINDOWS, 128)


def synthesis_table():
    ang = angles(T // FACES).T
    c, s = np.cos(ang) / math.sqrt(BINS), -np.sin(ang) / math.sqrt(BINS)
    z = np.zeros_like(c)
    first = np.concatenate([c, z, s, z], axis=0)
    second = np.concatenate([z, c, z, s], axis=0)
    return np.concatenate([first, second], axis=1).astype(np.float32)


def turns(n):
    a = 2.0 * np.pi * np.arange(n) / n
    return np.concatenate([np.cos(a), np.sin(a)]).astype(np.float32)


def lanes(shape):
    return lax.broadcasted_iota(jnp.int32, shape, len(shape) - 1)


def rows(shape):
    return lax.broadcasted_iota(jnp.int32, shape, len(shape) - 2)


def window_kernel(count_hbm, slip_hbm, ids_hbm, table_hbm, out, count, slip, ids, table, sems):
    q = lax.axis_index("freq")
    copies = [
        pltpu.make_async_copy(count_hbm, count, sems.at[0]),
        pltpu.make_async_copy(ids_hbm, ids, sems.at[1]),
        pltpu.make_async_copy(slip_hbm, slip, sems.at[2]),
        pltpu.make_async_copy(table_hbm.at[q], table, sems.at[3]),
    ]
    for copy in copies:
        copy.start()
    for copy in copies:
        copy.wait()
    both = jnp.concatenate(split2(table[...]), axis=1)
    r = jnp.dot(slip[...], both, preferred_element_type=f32)
    x = r[:, :128] + r[:, 128:]
    out[0:CAP, :] = jnp.where(rows((CAP, 128)) < count[0], x, 0.0)
    out[ID_ROW:HOLD, :] = jnp.full((HOLD - ID_ROW, 128), -1.0, f32)
    out[CAP:ID_ROW, :] = jnp.zeros((ID_ROW - CAP, 128), f32)
    live = lanes((1, CAP)) < count[0]
    out[ID_ROW : ID_ROW + 1, 0:CAP] = jnp.where(live, ids[...].astype(f32), -1.0)


def route_kernel(held, out):
    core = lax.rem(lax.axis_index("patch"), 2).astype(f32)
    n = 16 * 24
    r = rows((n, 128))
    d = lax.shift_right_logical(r * 2731, 16)
    j = lax.shift_right_logical(r - 24 * d, 1)
    base = (96 * d + 4 * j).astype(f32)
    block = lax.shift_right_logical(lanes((HOLD, 256)), 5) % 4
    odd = lax.rem(lax.shift_right_logical(lanes((HOLD, 128)), 5), 2) == 1
    left, right_hi, right_lo = [], [], []
    for k in range(2):
        x = held[k]
        re = jnp.where(odd, pltpu.roll(x, 32, 1), x)
        im = jnp.where(odd, x, pltpu.roll(x, 96, 1))
        hi, lo = split2(jnp.concatenate([re, im], axis=1))
        hi, lo = hi.astype(f32), lo.astype(f32)
        owner = held[k, ID_ROW : ID_ROW + 1, :]
        ahead = owner - base - 48.0 * core
        pad = jnp.zeros((128 - HOLD, 256), f32)
        for b in range(4):
            left.append(jnp.where(ahead == float(b), 1.0, 0.0))
            right_hi.append(jnp.where(block == b, hi, 0.0))
            right_hi.append(pad)
            right_lo.append(jnp.where(block == b, lo, 0.0))
            right_lo.append(pad)
    lhs = jnp.concatenate(left, axis=1).astype(bf16)
    rhs_hi = jnp.concatenate(right_hi, axis=0).astype(bf16)
    rhs_lo = jnp.concatenate(right_lo, axis=0).astype(bf16)
    got = jnp.dot(lhs, rhs_hi, preferred_element_type=f32) + jnp.dot(
        lhs, rhs_lo, preferred_element_type=f32
    )
    even = lax.rem(r, 2) == 0
    out[...] = jnp.where(even, got[:, :128], got[:, 128:]).reshape(16, 24, 128)


def spread_kernel(got, out):
    total = jnp.sum(got[...], axis=0)
    out[...] = jnp.broadcast_to(total[None], out.shape)


def sublane_sums(parts):
    sub = rows((8, 128))
    dist = 4
    while dist >= 1:
        low = (lax.shift_right_logical(sub, dist.bit_length() - 1) % 2) == 0
        parts = [
            jnp.where(low, a, b) + pltpu.roll(jnp.where(low, b, a), dist, 0)
            if dist == 4
            else jnp.where(low, a, b)
            + jnp.where(
                low, pltpu.roll(a, 8 - dist, 0), pltpu.roll(b, dist, 0)
            )
            for a, b in zip(parts[: len(parts) // 2], parts[len(parts) // 2 :])
        ]
        dist //= 2
    return parts[0]


def moment_kernel(green, moments, out, weights):
    spread = jnp.where(
        rows((OWN, OWN * BINS)) == lax.shift_right_logical(lanes((OWN, OWN * BINS)), 5),
        1.0,
        0.0,
    ).astype(bf16)
    hi, lo = split2(moments[...])
    w = jnp.dot(hi, spread, preferred_element_type=f32) + jnp.dot(
        lo, spread, preferred_element_type=f32
    )
    for m in range(6):
        weights[m] = jnp.broadcast_to(w[m : m + 1], (2, OWN * BINS))
    n_rows = 3 * STA_DEV
    for i in range(0, n_rows, 8):
        n = min(8, n_rows - i)
        acc = None
        for m in range(6):
            at = m * n_rows + i
            term = green[at : at + n].astype(f32) * weights[m][None]
            acc = term if acc is None else acc + term
        for j in range(12):
            out[i : i + n, 2 * j : 2 * j + 2, :] = acc[:, :, 128 * j : 128 * j + 128]


def patch_kernel(tiles, got, out):
    s = jnp.sum(got[...], axis=0)
    even = lax.rem(rows((24, 128)), 2) == 0
    for_re = jnp.where(even, s, -s)
    for_im = jnp.where(even, pltpu.roll(s, 23, 0), pltpu.roll(s, 1, 0))
    lane = lanes((8, 128))
    half = lane < 64
    block_even = lax.rem(lax.shift_right_logical(lane, 5), 2) == 0
    folded = []
    for c in range(3):
        for s0 in range(0, 32, 8):
            n = min(8, STA_DEV - s0)
            at = c * STA_DEV + s0
            acc = tiles[at : at + n]
            sums = []
            for weight in (for_re, for_im):
                p = (acc * weight[None]).reshape(n, 3, 8, 128)
                p = p[:, 0] + p[:, 1] + p[:, 2]
                parts = [p[i] for i in range(n)] + [jnp.zeros((8, 128), f32)] * (8 - n)
                sums.append(sublane_sums(parts))
            a, b = sums
            folded.append(
                jnp.where(half, a, b) + pltpu.roll(jnp.where(half, b, a), 64, 1)
            )
    for i in range(6):
        a, b = folded[i], folded[i + 6]
        w = jnp.where(block_even, a, b)
        z = jnp.where(block_even, pltpu.roll(a, 96, 1), pltpu.roll(b, 32, 1))
        out[8 * i : 8 * i + 8, :] = w + z


def spread_half_kernel(got, out):
    total = jnp.sum(got[...], axis=0).astype(bf16)
    out[...] = jnp.broadcast_to(total[None], out.shape)


def series_kernel(turn, got, table, out):
    p = lax.axis_index("patch")
    x = jnp.sum(got[...].astype(f32), axis=0)
    other = pltpu.roll(x, 64, 1)
    real = lanes((48, 128)) < 64
    x = turn[p] * x + turn[p + FACES] * jnp.where(real, -other, other)
    hi, lo = split2(x)
    lhs = jnp.concatenate([hi, lo, hi], axis=1)
    t_hi, t_lo = split2(table[...])
    rhs = jnp.concatenate([t_hi, t_hi, t_lo], axis=0)
    y = jnp.dot(lhs, rhs, preferred_element_type=f32)
    y = jnp.concatenate([y[:, :128], y[:, 128:]], axis=0)
    for c in range(3):
        out[c] = y[32 * c : 32 * c + STA_DEV]


VMEM = pl.BlockSpec(memory_space=pltpu.VMEM)
SMEM = pl.BlockSpec(memory_space=pltpu.SMEM)


HBM = pl.BlockSpec(memory_space=pltpu.HBM)


def call(kernel, shape, specs, *args, dtype=f32, scratch=(), grant=32):
    return pl.pallas_call(
        kernel,
        out_shape=jax.ShapeDtypeStruct(shape, dtype),
        in_specs=specs,
        out_specs=VMEM,
        scratch_shapes=scratch,
        compiler_params=pltpu.CompilerParams(vmem_limit_bytes=grant * 1024 * 1024),
    )(*args)


def local(slip_rate, face_counts, patch_ids, moments, green):
    held = call(
        window_kernel,
        (HOLD, 128),
        [HBM] * 4,
        face_counts,
        slip_rate,
        patch_ids.reshape(1, CAP),
        jnp.asarray(analysis_table()),
        scratch=[
            pltpu.SMEM((1,), jnp.int32),
            pltpu.VMEM((CAP, T // WINDOWS), bf16),
            pltpu.VMEM((1, CAP), jnp.int32),
            pltpu.VMEM((T // WINDOWS, 128), f32),
            pltpu.SemaphoreType.DMA((4,)),
        ],
        grant=60,
    )
    held = lax.all_gather(held, "patch", axis_index_groups=CORE_PAIRS)
    blocks = call(route_kernel, (16, 24, 128), [VMEM], held)
    blocks = lax.all_to_all(
        blocks, "patch", 0, 0, axis_index_groups=SAME_CORE, tiled=True
    )
    copies = call(spread_kernel, (16, 24, 128), [VMEM], blocks)
    copies = lax.all_to_all(copies, "freq", 0, 0, tiled=True)
    green = green.transpose(0, 2, 3, 1, 4).reshape(6 * 3 * STA_DEV, 2, OWN * BINS)
    tiles = call(
        moment_kernel,
        (3 * STA_DEV, 24, 128),
        [VMEM, VMEM],
        green,
        moments.T,
        scratch=[pltpu.VMEM((6, 2, OWN * BINS), f32)],
    )
    partial = call(patch_kernel, (48, 128), [VMEM, VMEM], tiles, copies)
    pair = lax.all_gather(partial, "patch", axis_index_groups=CORE_PAIRS)
    copies = call(spread_half_kernel, (16, 48, 128), [VMEM], pair, dtype=bf16)
    copies = lax.all_to_all(
        copies, "patch", 0, 0, axis_index_groups=SAME_CORE, tiled=True
    )
    return call(
        series_kernel,
        (3, STA_DEV, 128),
        [SMEM, VMEM, VMEM],
        jnp.asarray(turns(FACES)),
        copies,
        jnp.asarray(synthesis_table()),
    )


def solution(mesh):
    return jax.shard_map(
        local,
        mesh=mesh,
        in_specs=(
            P("patch", "freq"),
            P("patch"),
            P("patch"),
            P("patch", None),
            P(None, None, None, "freq", "patch"),
        ),
        out_specs=P(None, "freq", "patch"),
        check_vma=False,
    )
```

```python
import functools
import math

import jax
import jax.numpy as jnp
import numpy as np
from jax import lax
from jax.experimental import pallas as pl
from jax.experimental.pallas import tpu as pltpu
from jax.sharding import PartitionSpec as P

T = 4096
BINS = 32
FACES = 32
WINDOWS = 16
CAP = 84
OWN = 48
STA_DEV = 31
HOLD = 96
ID_ROW = 88

CORE_PAIRS = [[2 * d, 2 * d + 1] for d in range(16)]
SAME_CORE = [[2 * d + c for d in range(16)] for c in range(2)]
SAME_CORE_Z = [[16 * x + 2 * z + c for z in range(8) for x in range(2)] for c in range(2)]

CODE_SCALE = 2.0**56

f32 = jnp.float32
bf16 = jnp.bfloat16
f16 = jnp.float16


def split2(x):
    hi = x.astype(bf16)
    return hi, (x - hi.astype(f32)).astype(bf16)


def angles(samples):
    k = 1 + np.arange(BINS) * (T // (2 * BINS))
    return 2.0 * np.pi * ((np.arange(samples)[:, None] * k[None, :]) % T) / T


def analysis_table():
    t = np.arange(T)[:, None]
    k = 1 + np.arange(BINS) * (T // (2 * BINS))
    ang = 2.0 * np.pi * ((t * k) % T) / T
    c, s = np.cos(ang) / math.sqrt(T), -np.sin(ang) / math.sqrt(T)
    table = np.concatenate([c, s, c, s], axis=1).astype(np.float32)
    return table.reshape(WINDOWS, T // WINDOWS, 128)


def synthesis_table():
    ang = angles(T // FACES).T
    c, s = np.cos(ang) / math.sqrt(BINS), -np.sin(ang) / math.sqrt(BINS)
    z = np.zeros_like(c)
    first = np.concatenate([c, z, s, z], axis=0)
    second = np.concatenate([z, c, z, s], axis=0)
    return np.concatenate([first, second], axis=1).astype(np.float32)


def turns(n):
    a = 2.0 * np.pi * np.arange(n) / n
    both = np.stack([np.cos(a), np.sin(a)], axis=1).astype(np.float32)
    return np.broadcast_to(both[:, :, None], (n, 2, 128)).copy()


def lanes(shape):
    return lax.broadcasted_iota(jnp.int32, shape, len(shape) - 1)


def rows(shape):
    return lax.broadcasted_iota(jnp.int32, shape, len(shape) - 2)


def encode(x):
    root = jnp.sqrt(jnp.sqrt(jnp.abs(x) * CODE_SCALE))
    return jnp.where(x < 0.0, -root, root)


def decode(code):
    square = code * code
    return jnp.where(code < 0.0, -square, square) * square * (1.0 / CODE_SCALE)


def window_kernel(count_hbm, slip_hbm, ids_hbm, table_hbm, out, count, slip, ids, table, sems):
    q = lax.axis_index("freq")
    copies = [
        pltpu.make_async_copy(table_hbm.at[q], table, sems.at[0]),
        pltpu.make_async_copy(slip_hbm, slip, sems.at[1]),
        pltpu.make_async_copy(ids_hbm, ids, sems.at[2]),
        pltpu.make_async_copy(count_hbm, count, sems.at[3]),
    ]
    for copy in copies:
        copy.start()
    out[CAP:ID_ROW, :] = jnp.zeros((ID_ROW - CAP, 128), f32)
    out[ID_ROW:HOLD, :] = jnp.full((HOLD - ID_ROW, 128), -1.0, f32)
    for copy in copies:
        copy.wait()
    both = jnp.concatenate(split2(table[...]), axis=1)
    r = jnp.dot(slip[...], both, preferred_element_type=f32)
    out[0:CAP, :] = encode(r[:, :128] + r[:, 128:])
    live = lanes((1, CAP)) < count[...]
    out[ID_ROW : ID_ROW + 1, 0:CAP] = jnp.where(live, ids[...].astype(f32), -1.0)


def route_kernel(held, out):
    core = lax.rem(lax.axis_index("patch"), 2).astype(f32)
    n = 16 * 24
    r = rows((n, 128))
    d = lax.shift_right_logical(r * 2731, 16)
    j = lax.shift_right_logical(r - 24 * d, 1)
    base = (768 * (d & 1) + 96 * lax.shift_right_logical(d, 1) + 4 * j).astype(f32)
    base = base + 48.0 * core
    block = lax.shift_right_logical(lanes((HOLD, 256)), 5) % 4
    odd = lax.rem(lax.shift_right_logical(lanes((HOLD, 128)), 5), 2) == 1
    pad = jnp.zeros((128 - HOLD, 256), f32)
    left, right_hi, right_lo = [], [], []
    for k in range(2):
        x = held[k]
        re = jnp.where(odd, pltpu.roll(x, 32, 1), x)
        im = jnp.where(odd, x, pltpu.roll(x, 96, 1))
        hi, lo = split2(jnp.concatenate([re, im], axis=1))
        hi, lo = hi.astype(f32), lo.astype(f32)
        ahead = held[k, ID_ROW : ID_ROW + 1, :] - base
        for b in range(4):
            left.append(jnp.where(ahead == float(b), 1.0, 0.0))
            right_hi += [jnp.where(block == b, hi, 0.0), pad]
            right_lo += [jnp.where(block == b, lo, 0.0), pad]
    lhs = jnp.concatenate(left, axis=1).astype(bf16)
    rhs_hi = jnp.concatenate(right_hi, axis=0).astype(bf16)
    rhs_lo = jnp.concatenate(right_lo, axis=0).astype(bf16)
    got = jnp.dot(lhs, rhs_hi, preferred_element_type=f32) + jnp.dot(
        lhs, rhs_lo, preferred_element_type=f32
    )
    even = lax.rem(r, 2) == 0
    out[...] = jnp.where(even, got[:, :128], got[:, 128:]).reshape(16, 24, 128)


def sublane_sums(parts):
    sub = rows((8, 128))
    dist = 4
    while dist >= 1:
        low = (lax.shift_right_logical(sub, dist.bit_length() - 1) % 2) == 0
        parts = [
            jnp.where(low, a, b) + pltpu.roll(jnp.where(low, b, a), dist, 0)
            if dist == 4
            else jnp.where(low, a, b)
            + jnp.where(
                low, pltpu.roll(a, 8 - dist, 0), pltpu.roll(b, dist, 0)
            )
            for a, b in zip(parts[: len(parts) // 2], parts[len(parts) // 2 :])
        ]
        dist //= 2
    return parts[0]


def moment_kernel(green, moments, out, weights):
    spread = jnp.where(
        rows((OWN, OWN * BINS)) == lax.shift_right_logical(lanes((OWN, OWN * BINS)), 5),
        1.0,
        0.0,
    ).astype(bf16)
    hi, lo = split2(moments[...])
    w = jnp.dot(hi, spread, preferred_element_type=f32) + jnp.dot(
        lo, spread, preferred_element_type=f32
    )
    for m in range(6):
        weights[m] = jnp.broadcast_to(w[m : m + 1], (2, OWN * BINS))
    n_rows = 3 * STA_DEV
    for i in range(0, n_rows, 8):
        n = min(8, n_rows - i)
        acc = None
        for m in range(6):
            at = m * n_rows + i
            term = green[at : at + n].astype(f32) * weights[m][None]
            acc = term if acc is None else acc + term
        for j in range(12):
            out[i : i + n, 2 * j : 2 * j + 2, :] = acc[:, :, 128 * j : 128 * j + 128]


def patch_kernel(tiles, got, out):
    s = got[...]
    even = lax.rem(rows((24, 128)), 2) == 0
    for_re = jnp.where(even, s, -s)
    for_im = jnp.where(even, pltpu.roll(s, 23, 0), pltpu.roll(s, 1, 0))
    lane = lanes((8, 128))
    half = lane < 64
    block_even = lax.rem(lax.shift_right_logical(lane, 5), 2) == 0
    folded = []
    for c in range(3):
        for s0 in range(0, 32, 8):
            n = min(8, STA_DEV - s0)
            at = c * STA_DEV + s0
            acc = tiles[at : at + n]
            sums = []
            for weight in (for_re, for_im):
                p = (acc * weight[None]).reshape(n, 3, 8, 128)
                p = p[:, 0] + p[:, 1] + p[:, 2]
                parts = [p[i] for i in range(n)] + [jnp.zeros((8, 128), f32)] * (8 - n)
                sums.append(sublane_sums(parts))
            a, b = sums
            folded.append(
                jnp.where(half, a, b) + pltpu.roll(jnp.where(half, b, a), 64, 1)
            )
    for i in range(6):
        a, b = folded[i], folded[i + 6]
        w = jnp.where(block_even, a, b)
        z = jnp.where(block_even, pltpu.roll(a, 96, 1), pltpu.roll(b, 32, 1))
        out[8 * i : 8 * i + 8, :] = w + z


def spread_half_kernel(got, out):
    total = jnp.sum(got[...], axis=0).astype(bf16)
    out[...] = jnp.broadcast_to(total[None], out.shape)


def series_kernel(turn, got, table, out):
    p = lax.axis_index("patch")
    x = jnp.sum(got[...].astype(f32), axis=0)
    other = pltpu.roll(x, 64, 1)
    real = lanes((48, 128)) < 64
    turned = turn[p]
    x = turned[0:1] * x + turned[1:2] * jnp.where(real, -other, other)
    hi, lo = split2(x)
    lhs = jnp.concatenate([hi, lo, hi], axis=1)
    t_hi, t_lo = split2(table[...])
    rhs = jnp.concatenate([t_hi, t_hi, t_lo], axis=0)
    y = jnp.dot(lhs, rhs, preferred_element_type=f32)
    y = jnp.concatenate([y[:, :128], y[:, 128:]], axis=0)
    for c in range(3):
        out[c] = y[32 * c : 32 * c + STA_DEV]


VMEM = pl.BlockSpec(memory_space=pltpu.VMEM)
SMEM = pl.BlockSpec(memory_space=pltpu.SMEM)


HBM = pl.BlockSpec(memory_space=pltpu.HBM)


def call(kernel, shape, specs, *args, dtype=f32, scratch=(), grant=32):
    return pl.pallas_call(
        kernel,
        out_shape=jax.ShapeDtypeStruct(shape, dtype),
        in_specs=specs,
        out_specs=VMEM,
        scratch_shapes=scratch,
        compiler_params=pltpu.CompilerParams(vmem_limit_bytes=grant * 1024 * 1024),
    )(*args)


def local(slip_rate, face_counts, patch_ids, moments, green):
    held = call(
        window_kernel,
        (HOLD, 128),
        [HBM] * 4,
        face_counts.reshape(1, 1),
        slip_rate,
        patch_ids.reshape(1, CAP),
        jnp.asarray(analysis_table()),
        scratch=[
            pltpu.VMEM((1, 1), jnp.int32),
            pltpu.VMEM((CAP, T // WINDOWS), bf16),
            pltpu.VMEM((1, CAP), jnp.int32),
            pltpu.VMEM((T // WINDOWS, 128), f32),
            pltpu.SemaphoreType.DMA((4,)),
        ],
        grant=60,
    )
    held = lax.all_gather(held, "patch", axis_index_groups=CORE_PAIRS)
    blocks = call(route_kernel, (16, 24, 128), [VMEM], held).astype(f16)
    blocks = lax.all_to_all(
        blocks, "patch", 0, 0, axis_index_groups=SAME_CORE_Z, tiled=True
    )
    code = jnp.sum(blocks.astype(f32), axis=0).astype(f16)
    codes = jnp.broadcast_to(code[None], (WINDOWS, 24, 128))
    codes = lax.all_to_all(codes, "freq", 0, 0, tiled=True)
    spectra = jnp.sum(decode(codes.astype(f32)), axis=0)
    green = green.transpose(0, 2, 3, 1, 4).reshape(6 * 3 * STA_DEV, 2, OWN * BINS)
    tiles = call(
        moment_kernel,
        (3 * STA_DEV, 24, 128),
        [VMEM, VMEM],
        green,
        moments.T,
        scratch=[pltpu.VMEM((6, 2, OWN * BINS), f32)],
    )
    partial = call(patch_kernel, (48, 128), [VMEM, VMEM], tiles, spectra)
    pair = lax.all_gather(partial, "patch", axis_index_groups=CORE_PAIRS)
    copies = call(spread_half_kernel, (16, 48, 128), [VMEM], pair, dtype=bf16)
    copies = lax.all_to_all(
        copies, "patch", 0, 0, axis_index_groups=SAME_CORE, tiled=True
    )
    return call(
        series_kernel,
        (3, STA_DEV, 128),
        [VMEM, VMEM, VMEM],
        jnp.asarray(turns(FACES)),
        copies,
        jnp.asarray(synthesis_table()),
    )


def solution(mesh):
    return jax.shard_map(
        local,
        mesh=mesh,
        in_specs=(
            P("patch", "freq"),
            P("patch"),
            P("patch"),
            P("patch", None),
            P(None, None, None, "freq", "patch"),
        ),
        out_specs=P(None, "freq", "patch"),
        check_vma=False,
    )
```

```python
import functools
import math

import jax
import jax.numpy as jnp
import numpy as np
from jax import lax
from jax.experimental import pallas as pl
from jax.experimental.pallas import tpu as pltpu
from jax.sharding import PartitionSpec as P

T = 4096
BINS = 32
FACES = 32
WINDOWS = 16
CAP = 84
OWN = 48
STA_DEV = 31
HOLD = 96
ID_ROW = 88

CORE_PAIRS = [[2 * d, 2 * d + 1] for d in range(16)]
SAME_CORE = [[2 * d + c for d in range(16)] for c in range(2)]
SAME_CORE_Z = [[16 * x + 2 * z + c for z in range(8) for x in range(2)] for c in range(2)]
DOWN_Y = [4, 3, 2, 1, 0, 7, 6, 5]
WINDOW_GROUP = [[2 * y + x for x in range(2) for y in DOWN_Y]]

CODE_SCALE = 2.0**56

f32 = jnp.float32
bf16 = jnp.bfloat16
f16 = jnp.float16


def split2(x):
    hi = x.astype(bf16)
    return hi, (x - hi.astype(f32)).astype(bf16)


def angles(samples):
    k = 1 + np.arange(BINS) * (T // (2 * BINS))
    return 2.0 * np.pi * ((np.arange(samples)[:, None] * k[None, :]) % T) / T


def analysis_table():
    t = np.arange(T)[:, None]
    k = 1 + np.arange(BINS) * (T // (2 * BINS))
    ang = 2.0 * np.pi * ((t * k) % T) / T
    c, s = np.cos(ang) / math.sqrt(T), -np.sin(ang) / math.sqrt(T)
    table = np.concatenate([c, s, c, s], axis=1).astype(np.float32)
    return table.reshape(WINDOWS, T // WINDOWS, 128)


def synthesis_table():
    ang = angles(T // FACES).T
    c, s = np.cos(ang) / math.sqrt(BINS), -np.sin(ang) / math.sqrt(BINS)
    z = np.zeros_like(c)
    first = np.concatenate([c, z, s, z], axis=0)
    second = np.concatenate([z, c, z, s], axis=0)
    return np.concatenate([first, second], axis=1).astype(np.float32)


def turns(n):
    a = 2.0 * np.pi * np.arange(n) / n
    both = np.stack([np.cos(a), np.sin(a)], axis=1).astype(np.float32)
    return np.broadcast_to(both[:, :, None], (n, 2, 128)).copy()


def lanes(shape):
    return lax.broadcasted_iota(jnp.int32, shape, len(shape) - 1)


def rows(shape):
    return lax.broadcasted_iota(jnp.int32, shape, len(shape) - 2)


def encode(x):
    root = jnp.sqrt(jnp.sqrt(jnp.abs(x) * CODE_SCALE))
    return jnp.where(x < 0.0, -root, root)


def decode(code):
    square = code * code
    return jnp.where(code < 0.0, -square, square) * square * (1.0 / CODE_SCALE)


def window_kernel(count_hbm, slip_hbm, ids_hbm, table_hbm, out, count, slip, ids, table, sems):
    q = lax.axis_index("freq")
    copies = [
        pltpu.make_async_copy(table_hbm.at[q], table, sems.at[0]),
        pltpu.make_async_copy(slip_hbm, slip, sems.at[1]),
        pltpu.make_async_copy(ids_hbm, ids, sems.at[2]),
        pltpu.make_async_copy(count_hbm, count, sems.at[3]),
    ]
    for copy in copies:
        copy.start()
    out[CAP:ID_ROW, :] = jnp.zeros((ID_ROW - CAP, 128), f32)
    out[ID_ROW:HOLD, :] = jnp.full((HOLD - ID_ROW, 128), -1.0, f32)
    for copy in copies:
        copy.wait()
    both = jnp.concatenate(split2(table[...]), axis=1)
    r = jnp.dot(slip[...], both, preferred_element_type=f32)
    out[0:CAP, :] = encode(r[:, :128] + r[:, 128:])
    live = lanes((1, CAP)) < count[...]
    out[ID_ROW : ID_ROW + 1, 0:CAP] = jnp.where(live, ids[...].astype(f32), -1.0)


def route_kernel(held, out):
    core = lax.rem(lax.axis_index("patch"), 2).astype(f32)
    n = 16 * 24
    r = rows((n, 128))
    d = lax.shift_right_logical(r * 2731, 16)
    j = lax.shift_right_logical(r - 24 * d, 1)
    base = (768 * (d & 1) + 96 * lax.shift_right_logical(d, 1) + 4 * j).astype(f32)
    base = base + 48.0 * core
    block = lax.shift_right_logical(lanes((HOLD, 256)), 5) % 4
    odd = lax.rem(lax.shift_right_logical(lanes((HOLD, 128)), 5), 2) == 1
    pad = jnp.zeros((128 - HOLD, 256), f32)
    left, right_hi, right_lo = [], [], []
    for k in range(2):
        x = held[k]
        re = jnp.where(odd, pltpu.roll(x, 32, 1), x)
        im = jnp.where(odd, x, pltpu.roll(x, 96, 1))
        hi, lo = split2(jnp.concatenate([re, im], axis=1))
        hi, lo = hi.astype(f32), lo.astype(f32)
        ahead = held[k, ID_ROW : ID_ROW + 1, :] - base
        for b in range(4):
            left.append(jnp.where(ahead == float(b), 1.0, 0.0))
            right_hi += [jnp.where(block == b, hi, 0.0), pad]
            right_lo += [jnp.where(block == b, lo, 0.0), pad]
    lhs = jnp.concatenate(left, axis=1).astype(bf16)
    rhs_hi = jnp.concatenate(right_hi, axis=0).astype(bf16)
    rhs_lo = jnp.concatenate(right_lo, axis=0).astype(bf16)
    got = jnp.dot(lhs, rhs_hi, preferred_element_type=f32) + jnp.dot(
        lhs, rhs_lo, preferred_element_type=f32
    )
    even = lax.rem(r, 2) == 0
    out[...] = jnp.where(even, got[:, :128], got[:, 128:]).reshape(16, 24, 128)


def sublane_sums(parts):
    sub = rows((8, 128))
    dist = 4
    while dist >= 1:
        low = (lax.shift_right_logical(sub, dist.bit_length() - 1) % 2) == 0
        parts = [
            jnp.where(low, a, b) + pltpu.roll(jnp.where(low, b, a), dist, 0)
            if dist == 4
            else jnp.where(low, a, b)
            + jnp.where(
                low, pltpu.roll(a, 8 - dist, 0), pltpu.roll(b, dist, 0)
            )
            for a, b in zip(parts[: len(parts) // 2], parts[len(parts) // 2 :])
        ]
        dist //= 2
    return parts[0]


def moment_kernel(green, moments, out, weights):
    spread = jnp.where(
        rows((OWN, OWN * BINS)) == lax.shift_right_logical(lanes((OWN, OWN * BINS)), 5),
        1.0,
        0.0,
    ).astype(bf16)
    hi, lo = split2(moments[...])
    w = jnp.dot(hi, spread, preferred_element_type=f32) + jnp.dot(
        lo, spread, preferred_element_type=f32
    )
    for m in range(6):
        weights[m] = jnp.broadcast_to(w[m : m + 1], (2, OWN * BINS))
    n_rows = 3 * STA_DEV
    for i in range(0, n_rows, 8):
        n = min(8, n_rows - i)
        acc = None
        for m in range(6):
            at = m * n_rows + i
            term = green[at : at + n].astype(f32) * weights[m][None]
            acc = term if acc is None else acc + term
        for j in range(12):
            out[i : i + n, 2 * j : 2 * j + 2, :] = acc[:, :, 128 * j : 128 * j + 128]


def patch_kernel(tiles, got, out):
    s = got[...]
    even = lax.rem(rows((24, 128)), 2) == 0
    for_re = jnp.where(even, s, -s)
    for_im = jnp.where(even, pltpu.roll(s, 23, 0), pltpu.roll(s, 1, 0))
    lane = lanes((8, 128))
    half = lane < 64
    block_even = lax.rem(lax.shift_right_logical(lane, 5), 2) == 0
    folded = []
    for c in range(3):
        for s0 in range(0, 32, 8):
            n = min(8, STA_DEV - s0)
            at = c * STA_DEV + s0
            acc = tiles[at : at + n]
            sums = []
            for weight in (for_re, for_im):
                p = (acc * weight[None]).reshape(n, 3, 8, 128)
                p = p[:, 0] + p[:, 1] + p[:, 2]
                parts = [p[i] for i in range(n)] + [jnp.zeros((8, 128), f32)] * (8 - n)
                sums.append(sublane_sums(parts))
            a, b = sums
            folded.append(
                jnp.where(half, a, b) + pltpu.roll(jnp.where(half, b, a), 64, 1)
            )
    for i in range(6):
        a, b = folded[i], folded[i + 6]
        w = jnp.where(block_even, a, b)
        z = jnp.where(block_even, pltpu.roll(a, 96, 1), pltpu.roll(b, 32, 1))
        out[8 * i : 8 * i + 8, :] = w + z


def spread_half_kernel(got, out):
    total = jnp.sum(got[...], axis=0).astype(bf16)
    out[...] = jnp.broadcast_to(total[None], out.shape)


def series_kernel(turn, got, table, out):
    p = lax.axis_index("patch")
    x = jnp.sum(got[...].astype(f32), axis=0)
    other = pltpu.roll(x, 64, 1)
    real = lanes((48, 128)) < 64
    turned = turn[p]
    x = turned[0:1] * x + turned[1:2] * jnp.where(real, -other, other)
    hi, lo = split2(x)
    lhs = jnp.concatenate([hi, lo, hi], axis=1)
    t_hi, t_lo = split2(table[...])
    rhs = jnp.concatenate([t_hi, t_hi, t_lo], axis=0)
    y = jnp.dot(lhs, rhs, preferred_element_type=f32)
    y = jnp.concatenate([y[:, :128], y[:, 128:]], axis=0)
    for c in range(3):
        out[c] = y[32 * c : 32 * c + STA_DEV]


VMEM = pl.BlockSpec(memory_space=pltpu.VMEM)
SMEM = pl.BlockSpec(memory_space=pltpu.SMEM)


HBM = pl.BlockSpec(memory_space=pltpu.HBM)


def call(kernel, shape, specs, *args, dtype=f32, scratch=(), grant=32):
    return pl.pallas_call(
        kernel,
        out_shape=jax.ShapeDtypeStruct(shape, dtype),
        in_specs=specs,
        out_specs=VMEM,
        scratch_shapes=scratch,
        compiler_params=pltpu.CompilerParams(vmem_limit_bytes=grant * 1024 * 1024),
    )(*args)


def local(slip_rate, face_counts, patch_ids, moments, green):
    held = call(
        window_kernel,
        (HOLD, 128),
        [HBM] * 4,
        face_counts.reshape(1, 1),
        slip_rate,
        patch_ids.reshape(1, CAP),
        jnp.asarray(analysis_table()),
        scratch=[
            pltpu.VMEM((1, 1), jnp.int32),
            pltpu.VMEM((CAP, T // WINDOWS), bf16),
            pltpu.VMEM((1, CAP), jnp.int32),
            pltpu.VMEM((T // WINDOWS, 128), f32),
            pltpu.SemaphoreType.DMA((4,)),
        ],
        grant=60,
    )
    held = lax.all_gather(held, "patch", axis_index_groups=CORE_PAIRS)
    blocks = call(route_kernel, (16, 24, 128), [VMEM], held).astype(f16)
    blocks = lax.all_to_all(
        blocks, "patch", 0, 0, axis_index_groups=SAME_CORE_Z, tiled=True
    )
    code = jnp.sum(blocks.astype(f32), axis=0).astype(f16)
    codes = jnp.broadcast_to(code[None], (WINDOWS, 24, 128))
    codes = lax.all_to_all(
        codes, "freq", 0, 0, axis_index_groups=WINDOW_GROUP, tiled=True
    )
    spectra = jnp.sum(decode(codes.astype(f32)), axis=0)
    green = green.transpose(0, 2, 3, 1, 4).reshape(6 * 3 * STA_DEV, 2, OWN * BINS)
    tiles = call(
        moment_kernel,
        (3 * STA_DEV, 24, 128),
        [VMEM, VMEM],
        green,
        moments.T,
        scratch=[pltpu.VMEM((6, 2, OWN * BINS), f32)],
    )
    partial = call(patch_kernel, (48, 128), [VMEM, VMEM], tiles, spectra)
    pair = lax.all_gather(partial, "patch", axis_index_groups=CORE_PAIRS)
    copies = call(spread_half_kernel, (16, 48, 128), [VMEM], pair, dtype=bf16)
    copies = lax.all_to_all(
        copies, "patch", 0, 0, axis_index_groups=SAME_CORE, tiled=True
    )
    return call(
        series_kernel,
        (3, STA_DEV, 128),
        [VMEM, VMEM, VMEM],
        jnp.asarray(turns(FACES)),
        copies,
        jnp.asarray(synthesis_table()),
    )


def solution(mesh):
    return jax.shard_map(
        local,
        mesh=mesh,
        in_specs=(
            P("patch", "freq"),
            P("patch"),
            P("patch"),
            P("patch", None),
            P(None, None, None, "freq", "patch"),
        ),
        out_specs=P(None, "freq", "patch"),
        check_vma=False,
    )
```

```python
import functools
import math

import jax
import jax.numpy as jnp
import numpy as np
from jax import lax
from jax.experimental import pallas as pl
from jax.experimental.pallas import tpu as pltpu
from jax.sharding import PartitionSpec as P

T = 4096
BINS = 32
FACES = 32
WINDOWS = 16
CAP = 84
OWN = 48
STA_DEV = 31
HOLD = 96
ID_ROW = 88

CORE_PAIRS = [[2 * d, 2 * d + 1] for d in range(16)]
SAME_CORE = [[2 * d + c for d in range(16)] for c in range(2)]
DOWN_Y = [4, 3, 2, 1, 0, 7, 6, 5]
WINDOW_GROUP = [[2 * y + x for x in (1, 0) for y in DOWN_Y]]

CODE_SCALE = 2.0**56

f32 = jnp.float32
bf16 = jnp.bfloat16
f16 = jnp.float16


def split2(x):
    hi = x.astype(bf16)
    return hi, (x - hi.astype(f32)).astype(bf16)


def angles(samples):
    k = 1 + np.arange(BINS) * (T // (2 * BINS))
    return 2.0 * np.pi * ((np.arange(samples)[:, None] * k[None, :]) % T) / T


def analysis_table():
    t = np.arange(T)[:, None]
    k = 1 + np.arange(BINS) * (T // (2 * BINS))
    ang = 2.0 * np.pi * ((t * k) % T) / T
    c, s = np.cos(ang) / math.sqrt(T), -np.sin(ang) / math.sqrt(T)
    table = np.concatenate([c, s, c, s], axis=1).astype(np.float32)
    return table.reshape(WINDOWS, T // WINDOWS, 128)


def synthesis_table():
    ang = angles(T // FACES).T
    c, s = np.cos(ang) / math.sqrt(BINS), -np.sin(ang) / math.sqrt(BINS)
    z = np.zeros_like(c)
    first = np.concatenate([c, z, s, z], axis=0)
    second = np.concatenate([z, c, z, s], axis=0)
    return np.concatenate([first, second], axis=1).astype(np.float32)


def turns(n):
    a = 2.0 * np.pi * np.arange(n) / n
    both = np.stack([np.cos(a), np.sin(a)], axis=1).astype(np.float32)
    return np.broadcast_to(both[:, :, None], (n, 2, 128)).copy()


def lanes(shape):
    return lax.broadcasted_iota(jnp.int32, shape, len(shape) - 1)


def rows(shape):
    return lax.broadcasted_iota(jnp.int32, shape, len(shape) - 2)


def encode(x):
    root = jnp.sqrt(jnp.sqrt(jnp.abs(x) * CODE_SCALE))
    return jnp.where(x < 0.0, -root, root)


def decode(code):
    square = code * code
    return jnp.where(code < 0.0, -square, square) * square * (1.0 / CODE_SCALE)


def window_kernel(count_hbm, slip_hbm, ids_hbm, table_hbm, out, count, slip, ids, table, sems):
    q = lax.axis_index("freq")
    copies = [
        pltpu.make_async_copy(table_hbm.at[q], table, sems.at[0]),
        pltpu.make_async_copy(slip_hbm, slip, sems.at[1]),
        pltpu.make_async_copy(ids_hbm, ids, sems.at[2]),
        pltpu.make_async_copy(count_hbm, count, sems.at[3]),
    ]
    for copy in copies:
        copy.start()
    out[CAP:ID_ROW, :] = jnp.zeros((ID_ROW - CAP, 128), f32)
    out[ID_ROW:HOLD, :] = jnp.full((HOLD - ID_ROW, 128), -1.0, f32)
    for copy in copies:
        copy.wait()
    both = jnp.concatenate(split2(table[...]), axis=1)
    r = jnp.dot(slip[...], both, preferred_element_type=f32)
    out[0:CAP, :] = encode(r[:, :128] + r[:, 128:])
    live = lanes((1, CAP)) < count[...]
    out[ID_ROW : ID_ROW + 1, 0:CAP] = jnp.where(live, ids[...].astype(f32), -1.0)


def route_kernel(held, out):
    core = lax.rem(lax.axis_index("patch"), 2).astype(f32)
    n = 16 * 24
    r = rows((n, 128))
    d = lax.shift_right_logical(r * 2731, 16)
    j = lax.shift_right_logical(r - 24 * d, 1)
    base = (96 * d + 4 * j).astype(f32)
    base = base + 48.0 * core
    block = lax.shift_right_logical(lanes((HOLD, 256)), 5) % 4
    odd = lax.rem(lax.shift_right_logical(lanes((HOLD, 128)), 5), 2) == 1
    pad = jnp.zeros((128 - HOLD, 256), f32)
    left, right_hi, right_lo = [], [], []
    for k in range(2):
        x = held[k]
        re = jnp.where(odd, pltpu.roll(x, 32, 1), x)
        im = jnp.where(odd, x, pltpu.roll(x, 96, 1))
        hi, lo = split2(jnp.concatenate([re, im], axis=1))
        hi, lo = hi.astype(f32), lo.astype(f32)
        ahead = held[k, ID_ROW : ID_ROW + 1, :] - base
        for b in range(4):
            left.append(jnp.where(ahead == float(b), 1.0, 0.0))
            right_hi += [jnp.where(block == b, hi, 0.0), pad]
            right_lo += [jnp.where(block == b, lo, 0.0), pad]
    lhs = jnp.concatenate(left, axis=1).astype(bf16)
    rhs_hi = jnp.concatenate(right_hi, axis=0).astype(bf16)
    rhs_lo = jnp.concatenate(right_lo, axis=0).astype(bf16)
    got = jnp.dot(lhs, rhs_hi, preferred_element_type=f32) + jnp.dot(
        lhs, rhs_lo, preferred_element_type=f32
    )
    even = lax.rem(r, 2) == 0
    out[...] = jnp.where(even, got[:, :128], got[:, 128:]).reshape(16, 24, 128)


def sublane_sums(parts):
    sub = rows((8, 128))
    dist = 4
    while dist >= 1:
        low = (lax.shift_right_logical(sub, dist.bit_length() - 1) % 2) == 0
        parts = [
            jnp.where(low, a, b) + pltpu.roll(jnp.where(low, b, a), dist, 0)
            if dist == 4
            else jnp.where(low, a, b)
            + jnp.where(
                low, pltpu.roll(a, 8 - dist, 0), pltpu.roll(b, dist, 0)
            )
            for a, b in zip(parts[: len(parts) // 2], parts[len(parts) // 2 :])
        ]
        dist //= 2
    return parts[0]


def moment_kernel(green, moments, out, weights):
    spread = jnp.where(
        rows((OWN, OWN * BINS)) == lax.shift_right_logical(lanes((OWN, OWN * BINS)), 5),
        1.0,
        0.0,
    ).astype(bf16)
    hi, lo = split2(moments[...])
    w = jnp.dot(hi, spread, preferred_element_type=f32) + jnp.dot(
        lo, spread, preferred_element_type=f32
    )
    for m in range(6):
        weights[m] = jnp.broadcast_to(w[m : m + 1], (2, OWN * BINS))
    n_rows = 3 * STA_DEV
    for i in range(0, n_rows, 8):
        n = min(8, n_rows - i)
        acc = None
        for m in range(6):
            at = m * n_rows + i
            term = green[at : at + n].astype(f32) * weights[m][None]
            acc = term if acc is None else acc + term
        for j in range(12):
            out[i : i + n, 2 * j : 2 * j + 2, :] = acc[:, :, 128 * j : 128 * j + 128]


def patch_kernel(tiles, got, out):
    s = got[...]
    even = lax.rem(rows((24, 128)), 2) == 0
    for_re = jnp.where(even, s, -s)
    for_im = jnp.where(even, pltpu.roll(s, 23, 0), pltpu.roll(s, 1, 0))
    lane = lanes((8, 128))
    half = lane < 64
    block_even = lax.rem(lax.shift_right_logical(lane, 5), 2) == 0
    folded = []
    for c in range(3):
        for s0 in range(0, 32, 8):
            n = min(8, STA_DEV - s0)
            at = c * STA_DEV + s0
            acc = tiles[at : at + n]
            sums = []
            for weight in (for_re, for_im):
                p = (acc * weight[None]).reshape(n, 3, 8, 128)
                p = p[:, 0] + p[:, 1] + p[:, 2]
                parts = [p[i] for i in range(n)] + [jnp.zeros((8, 128), f32)] * (8 - n)
                sums.append(sublane_sums(parts))
            a, b = sums
            folded.append(
                jnp.where(half, a, b) + pltpu.roll(jnp.where(half, b, a), 64, 1)
            )
    for i in range(6):
        a, b = folded[i], folded[i + 6]
        w = jnp.where(block_even, a, b)
        z = jnp.where(block_even, pltpu.roll(a, 96, 1), pltpu.roll(b, 32, 1))
        out[8 * i : 8 * i + 8, :] = w + z


def spread_half_kernel(got, out):
    total = jnp.sum(got[...], axis=0).astype(bf16)
    out[...] = jnp.broadcast_to(total[None], out.shape)


def series_kernel(turn, got, table, out):
    p = lax.axis_index("patch")
    x = jnp.sum(got[...].astype(f32), axis=0)
    other = pltpu.roll(x, 64, 1)
    real = lanes((48, 128)) < 64
    turned = turn[p]
    x = turned[0:1] * x + turned[1:2] * jnp.where(real, -other, other)
    hi, lo = split2(x)
    lhs = jnp.concatenate([hi, lo, hi], axis=1)
    t_hi, t_lo = split2(table[...])
    rhs = jnp.concatenate([t_hi, t_hi, t_lo], axis=0)
    y = jnp.dot(lhs, rhs, preferred_element_type=f32)
    y = jnp.concatenate([y[:, :128], y[:, 128:]], axis=0)
    for c in range(3):
        out[c] = y[32 * c : 32 * c + STA_DEV]


VMEM = pl.BlockSpec(memory_space=pltpu.VMEM)
SMEM = pl.BlockSpec(memory_space=pltpu.SMEM)


HBM = pl.BlockSpec(memory_space=pltpu.HBM)


def call(kernel, shape, specs, *args, dtype=f32, scratch=(), grant=32):
    return pl.pallas_call(
        kernel,
        out_shape=jax.ShapeDtypeStruct(shape, dtype),
        in_specs=specs,
        out_specs=VMEM,
        scratch_shapes=scratch,
        compiler_params=pltpu.CompilerParams(vmem_limit_bytes=grant * 1024 * 1024),
    )(*args)


def local(slip_rate, face_counts, patch_ids, moments, green):
    held = call(
        window_kernel,
        (HOLD, 128),
        [HBM] * 4,
        face_counts.reshape(1, 1),
        slip_rate,
        patch_ids.reshape(1, CAP),
        jnp.asarray(analysis_table()),
        scratch=[
            pltpu.VMEM((1, 1), jnp.int32),
            pltpu.VMEM((CAP, T // WINDOWS), bf16),
            pltpu.VMEM((1, CAP), jnp.int32),
            pltpu.VMEM((T // WINDOWS, 128), f32),
            pltpu.SemaphoreType.DMA((4,)),
        ],
        grant=60,
    )
    held = lax.all_gather(held, "patch", axis_index_groups=CORE_PAIRS)
    blocks = call(route_kernel, (16, 24, 128), [VMEM], held).astype(f16)
    blocks = lax.all_to_all(
        blocks, "patch", 0, 0, axis_index_groups=SAME_CORE, tiled=True
    )
    code = jnp.sum(blocks.astype(f32), axis=0).astype(f16)
    codes = jnp.broadcast_to(code[None], (WINDOWS, 24, 128))
    codes = lax.all_to_all(
        codes, "freq", 0, 0, axis_index_groups=WINDOW_GROUP, tiled=True
    )
    spectra = jnp.sum(decode(codes.astype(f32)), axis=0)
    green = green.transpose(0, 2, 3, 1, 4).reshape(6 * 3 * STA_DEV, 2, OWN * BINS)
    tiles = call(
        moment_kernel,
        (3 * STA_DEV, 24, 128),
        [VMEM, VMEM],
        green,
        moments.T,
        scratch=[pltpu.VMEM((6, 2, OWN * BINS), f32)],
    )
    partial = call(patch_kernel, (48, 128), [VMEM, VMEM], tiles, spectra)
    pair = lax.all_gather(partial, "patch", axis_index_groups=CORE_PAIRS)
    copies = call(spread_half_kernel, (16, 48, 128), [VMEM], pair, dtype=bf16)
    copies = lax.all_to_all(
        copies, "patch", 0, 0, axis_index_groups=SAME_CORE, tiled=True
    )
    return call(
        series_kernel,
        (3, STA_DEV, 128),
        [VMEM, VMEM, VMEM],
        jnp.asarray(turns(FACES)),
        copies,
        jnp.asarray(synthesis_table()),
    )


def solution(mesh):
    return jax.shard_map(
        local,
        mesh=mesh,
        in_specs=(
            P("patch", "freq"),
            P("patch"),
            P("patch"),
            P("patch", None),
            P(None, None, None, "freq", "patch"),
        ),
        out_specs=P(None, "freq", "patch"),
        check_vma=False,
    )
```

```python
import functools
import math

import jax
import jax.numpy as jnp
import numpy as np
from jax import lax
from jax.experimental import pallas as pl
from jax.experimental.pallas import tpu as pltpu
from jax.sharding import PartitionSpec as P

T = 4096
BINS = 32
FACES = 32
WINDOWS = 16
CAP = 84
OWN = 48
STA_DEV = 31
HOLD = 96
ID_ROW = 88

CORE_PAIRS = [[2 * d, 2 * d + 1] for d in range(16)]
SAME_CORE = [[2 * d + c for d in range(16)] for c in range(2)]
DOWN_Y = [4, 3, 2, 1, 0, 7, 6, 5]
WINDOW_GROUP = [[2 * y + x for x in (1, 0) for y in DOWN_Y]]

CODE_SCALE = 2.0**56

f32 = jnp.float32
bf16 = jnp.bfloat16
f16 = jnp.float16


def split2(x):
    hi = x.astype(bf16)
    return hi, (x - hi.astype(f32)).astype(bf16)


def angles(samples):
    k = 1 + np.arange(BINS) * (T // (2 * BINS))
    return 2.0 * np.pi * ((np.arange(samples)[:, None] * k[None, :]) % T) / T


def analysis_table():
    t = np.arange(T)[:, None]
    k = 1 + np.arange(BINS) * (T // (2 * BINS))
    ang = 2.0 * np.pi * ((t * k) % T) / T
    c, s = np.cos(ang) / math.sqrt(T), -np.sin(ang) / math.sqrt(T)
    table = np.concatenate([c, s, c, s], axis=1).astype(np.float32)
    return table.reshape(WINDOWS, T // WINDOWS, 128)


def synthesis_table():
    ang = angles(T // FACES).T
    c, s = np.cos(ang) / math.sqrt(BINS), -np.sin(ang) / math.sqrt(BINS)
    z = np.zeros_like(c)
    first = np.concatenate([c, z, s, z], axis=0)
    second = np.concatenate([z, c, z, s], axis=0)
    return np.concatenate([first, second], axis=1).astype(np.float32)


def turns(n):
    a = 2.0 * np.pi * np.arange(n) / n
    both = np.stack([np.cos(a), np.sin(a)], axis=1).astype(np.float32)
    return np.broadcast_to(both[:, :, None], (n, 2, 128)).copy()


def lanes(shape):
    return lax.broadcasted_iota(jnp.int32, shape, len(shape) - 1)


def rows(shape):
    return lax.broadcasted_iota(jnp.int32, shape, len(shape) - 2)


def encode(x):
    root = jnp.sqrt(jnp.sqrt(jnp.abs(x) * CODE_SCALE))
    return jnp.where(x < 0.0, -root, root)


def decode(code):
    square = code * code
    return jnp.where(code < 0.0, -square, square) * square * (1.0 / CODE_SCALE)


def window_kernel(count_hbm, slip_hbm, ids_hbm, table_hbm, out, count, slip, ids, table, sems):
    q = lax.axis_index("freq")
    copies = [
        pltpu.make_async_copy(table_hbm.at[q], table, sems.at[0]),
        pltpu.make_async_copy(slip_hbm, slip, sems.at[1]),
        pltpu.make_async_copy(ids_hbm, ids, sems.at[2]),
        pltpu.make_async_copy(count_hbm, count, sems.at[3]),
    ]
    for copy in copies:
        copy.start()
    out[CAP:ID_ROW, :] = jnp.zeros((ID_ROW - CAP, 128), f32)
    out[ID_ROW:HOLD, :] = jnp.full((HOLD - ID_ROW, 128), -1.0, f32)
    for copy in copies:
        copy.wait()
    both = jnp.concatenate(split2(table[...]), axis=1)
    r = jnp.dot(slip[...], both, preferred_element_type=f32)
    out[0:CAP, :] = encode(r[:, :128] + r[:, 128:])
    live = lanes((1, CAP)) < count[...]
    out[ID_ROW : ID_ROW + 1, 0:CAP] = jnp.where(live, ids[...].astype(f32), -1.0)


def route_kernel(held, out):
    core = lax.rem(lax.axis_index("patch"), 2).astype(f32)
    n = 16 * 24
    r = rows((n, 128))
    d = lax.shift_right_logical(r * 2731, 16)
    j = lax.shift_right_logical(r - 24 * d, 1)
    base = (96 * d + 4 * j).astype(f32)
    base = base + 48.0 * core
    block = lax.shift_right_logical(lanes((HOLD, 256)), 5) % 4
    odd = lax.rem(lax.shift_right_logical(lanes((HOLD, 128)), 5), 2) == 1
    pad = jnp.zeros((128 - HOLD, 256), f32)
    left, right_hi, right_lo = [], [], []
    for k in range(2):
        x = held[k]
        re = jnp.where(odd, pltpu.roll(x, 32, 1), x)
        im = jnp.where(odd, x, pltpu.roll(x, 96, 1))
        hi, lo = split2(jnp.concatenate([re, im], axis=1))
        hi, lo = hi.astype(f32), lo.astype(f32)
        ahead = held[k, ID_ROW : ID_ROW + 1, :] - base
        for b in range(4):
            left.append(jnp.where(ahead == float(b), 1.0, 0.0))
            right_hi += [jnp.where(block == b, hi, 0.0), pad]
            right_lo += [jnp.where(block == b, lo, 0.0), pad]
    lhs = jnp.concatenate(left, axis=1).astype(bf16)
    rhs_hi = jnp.concatenate(right_hi, axis=0).astype(bf16)
    rhs_lo = jnp.concatenate(right_lo, axis=0).astype(bf16)
    got = jnp.dot(lhs, rhs_hi, preferred_element_type=f32) + jnp.dot(
        lhs, rhs_lo, preferred_element_type=f32
    )
    even = lax.rem(r, 2) == 0
    out[...] = jnp.where(even, got[:, :128], got[:, 128:]).reshape(16, 24, 128)


def sublane_sums(parts):
    sub = rows((8, 128))
    dist = 4
    while dist >= 1:
        low = (lax.shift_right_logical(sub, dist.bit_length() - 1) % 2) == 0
        parts = [
            jnp.where(low, a, b) + pltpu.roll(jnp.where(low, b, a), dist, 0)
            if dist == 4
            else jnp.where(low, a, b)
            + jnp.where(
                low, pltpu.roll(a, 8 - dist, 0), pltpu.roll(b, dist, 0)
            )
            for a, b in zip(parts[: len(parts) // 2], parts[len(parts) // 2 :])
        ]
        dist //= 2
    return parts[0]


def moment_kernel(green, moments, out, weights):
    spread = jnp.where(
        rows((OWN, OWN * BINS)) == lax.shift_right_logical(lanes((OWN, OWN * BINS)), 5),
        1.0,
        0.0,
    ).astype(bf16)
    hi, lo = split2(moments[...])
    w = jnp.dot(hi, spread, preferred_element_type=f32) + jnp.dot(
        lo, spread, preferred_element_type=f32
    )
    for m in range(6):
        weights[m] = jnp.broadcast_to(w[m : m + 1], (2, OWN * BINS))
    n_rows = 3 * STA_DEV
    for i in range(0, n_rows, 8):
        n = min(8, n_rows - i)
        acc = None
        for m in range(6):
            at = m * n_rows + i
            term = green[at : at + n].astype(f32) * weights[m][None]
            acc = term if acc is None else acc + term
        for j in range(12):
            out[i : i + n, 2 * j : 2 * j + 2, :] = acc[:, :, 128 * j : 128 * j + 128]


def patch_kernel(tiles, got, out):
    s = got[...]
    even = lax.rem(rows((24, 128)), 2) == 0
    for_re = jnp.where(even, s, -s)
    for_im = jnp.where(even, pltpu.roll(s, 23, 0), pltpu.roll(s, 1, 0))
    lane = lanes((8, 128))
    half = lane < 64
    block_even = lax.rem(lax.shift_right_logical(lane, 5), 2) == 0
    folded = []
    for c in range(3):
        for s0 in range(0, 32, 8):
            n = min(8, STA_DEV - s0)
            at = c * STA_DEV + s0
            acc = tiles[at : at + n]
            sums = []
            for weight in (for_re, for_im):
                p = (acc * weight[None]).reshape(n, 3, 8, 128)
                p = p[:, 0] + p[:, 1] + p[:, 2]
                parts = [p[i] for i in range(n)] + [jnp.zeros((8, 128), f32)] * (8 - n)
                sums.append(sublane_sums(parts))
            a, b = sums
            folded.append(
                jnp.where(half, a, b) + pltpu.roll(jnp.where(half, b, a), 64, 1)
            )
    for i in range(6):
        a, b = folded[i], folded[i + 6]
        w = jnp.where(block_even, a, b)
        z = jnp.where(block_even, pltpu.roll(a, 96, 1), pltpu.roll(b, 32, 1))
        out[8 * i : 8 * i + 8, :] = w + z


def spread_half_kernel(got, out):
    total = jnp.sum(got[...], axis=0).astype(bf16)
    out[...] = jnp.broadcast_to(total[None], out.shape)


def series_kernel(turn, got, table, out):
    p = lax.axis_index("patch")
    x = jnp.sum(got[...].astype(f32), axis=0)
    other = pltpu.roll(x, 64, 1)
    real = lanes((48, 128)) < 64
    turned = turn[p]
    x = turned[0:1] * x + turned[1:2] * jnp.where(real, -other, other)
    hi, lo = split2(x)
    lhs = jnp.concatenate([hi, lo, hi], axis=1)
    t_hi, t_lo = split2(table[...])
    rhs = jnp.concatenate([t_hi, t_hi, t_lo], axis=0)
    y = jnp.dot(lhs, rhs, preferred_element_type=f32)
    y = jnp.concatenate([y[:, :128], y[:, 128:]], axis=0)
    for c in range(3):
        out[c] = y[32 * c : 32 * c + STA_DEV]


VMEM = pl.BlockSpec(memory_space=pltpu.VMEM)
SMEM = pl.BlockSpec(memory_space=pltpu.SMEM)


HBM = pl.BlockSpec(memory_space=pltpu.HBM)


def call(kernel, shape, specs, *args, dtype=f32, scratch=(), grant=32):
    return pl.pallas_call(
        kernel,
        out_shape=jax.ShapeDtypeStruct(shape, dtype),
        in_specs=specs,
        out_specs=VMEM,
        scratch_shapes=scratch,
        compiler_params=pltpu.CompilerParams(vmem_limit_bytes=grant * 1024 * 1024),
    )(*args)


def local(slip_rate, face_counts, patch_ids, moments, green):
    held = call(
        window_kernel,
        (HOLD, 128),
        [HBM] * 4,
        face_counts.reshape(1, 1),
        slip_rate,
        patch_ids.reshape(1, CAP),
        jnp.asarray(analysis_table()),
        scratch=[
            pltpu.VMEM((1, 1), jnp.int32),
            pltpu.VMEM((CAP, T // WINDOWS), bf16),
            pltpu.VMEM((1, CAP), jnp.int32),
            pltpu.VMEM((T // WINDOWS, 128), f32),
            pltpu.SemaphoreType.DMA((4,)),
        ],
        grant=60,
    )
    held = lax.all_gather(held, "patch", axis_index_groups=CORE_PAIRS)
    blocks = call(route_kernel, (16, 24, 128), [VMEM], held).astype(f16)
    blocks = lax.all_to_all(
        blocks, "patch", 0, 0, axis_index_groups=SAME_CORE, tiled=True
    )
    green = green.transpose(0, 2, 3, 1, 4).reshape(6 * 3 * STA_DEV, 2, OWN * BINS)
    tiles = call(
        moment_kernel,
        (3 * STA_DEV, 24, 128),
        [VMEM, VMEM],
        green,
        moments.T,
        scratch=[pltpu.VMEM((6, 2, OWN * BINS), f32)],
    )
    code = jnp.sum(blocks.astype(f32), axis=0).astype(f16)
    code, tiles = lax.optimization_barrier((code, tiles))
    codes = jnp.broadcast_to(code[None], (WINDOWS, 24, 128))
    codes = lax.all_to_all(
        codes, "freq", 0, 0, axis_index_groups=WINDOW_GROUP, tiled=True
    )
    spectra = jnp.sum(decode(codes.astype(f32)), axis=0)
    partial = call(patch_kernel, (48, 128), [VMEM, VMEM], tiles, spectra)
    pair = lax.all_gather(partial, "patch", axis_index_groups=CORE_PAIRS)
    copies = call(spread_half_kernel, (16, 48, 128), [VMEM], pair, dtype=bf16)
    copies = lax.all_to_all(
        copies, "patch", 0, 0, axis_index_groups=SAME_CORE, tiled=True
    )
    return call(
        series_kernel,
        (3, STA_DEV, 128),
        [VMEM, VMEM, VMEM],
        jnp.asarray(turns(FACES)),
        copies,
        jnp.asarray(synthesis_table()),
    )


def solution(mesh):
    return jax.shard_map(
        local,
        mesh=mesh,
        in_specs=(
            P("patch", "freq"),
            P("patch"),
            P("patch"),
            P("patch", None),
            P(None, None, None, "freq", "patch"),
        ),
        out_specs=P(None, "freq", "patch"),
        check_vma=False,
    )
```

```python
import functools
import math

import jax
import jax.numpy as jnp
import numpy as np
from jax import lax
from jax.experimental import pallas as pl
from jax.experimental.pallas import tpu as pltpu
from jax.sharding import PartitionSpec as P

T = 4096
BINS = 32
FACES = 32
WINDOWS = 16
CAP = 84
OWN = 48
STA_DEV = 31
HOLD = 96
ID_ROW = 88

CORE_PAIRS = [[2 * d, 2 * d + 1] for d in range(16)]
SAME_CORE = [[2 * d + c for d in range(16)] for c in range(2)]
DOWN_Y = [4, 3, 2, 1, 0, 7, 6, 5]
WINDOW_GROUP = [[2 * y + x for x in (1, 0) for y in DOWN_Y]]

CODE_SCALE = 2.0**56

f32 = jnp.float32
bf16 = jnp.bfloat16
f16 = jnp.float16


def split2(x):
    hi = x.astype(bf16)
    return hi, (x - hi.astype(f32)).astype(bf16)


def angles(samples):
    k = 1 + np.arange(BINS) * (T // (2 * BINS))
    return 2.0 * np.pi * ((np.arange(samples)[:, None] * k[None, :]) % T) / T


def analysis_table():
    t = np.arange(T)[:, None]
    k = 1 + np.arange(BINS) * (T // (2 * BINS))
    ang = 2.0 * np.pi * ((t * k) % T) / T
    c, s = np.cos(ang) / math.sqrt(T), -np.sin(ang) / math.sqrt(T)
    table = np.concatenate([c, s, c, s], axis=1).astype(np.float32)
    return table.reshape(WINDOWS, T // WINDOWS, 128)


def synthesis_table():
    ang = angles(T // FACES).T
    c, s = np.cos(ang) / math.sqrt(BINS), -np.sin(ang) / math.sqrt(BINS)
    z = np.zeros_like(c)
    first = np.concatenate([c, z, s, z], axis=0)
    second = np.concatenate([z, c, z, s], axis=0)
    return np.concatenate([first, second], axis=1).astype(np.float32)


def turns(n):
    a = 2.0 * np.pi * np.arange(n) / n
    both = np.stack([np.cos(a), np.sin(a)], axis=1).astype(np.float32)
    return np.broadcast_to(both[:, :, None], (n, 2, 128)).copy()


def lanes(shape):
    return lax.broadcasted_iota(jnp.int32, shape, len(shape) - 1)


def rows(shape):
    return lax.broadcasted_iota(jnp.int32, shape, len(shape) - 2)


def encode(x):
    root = jnp.sqrt(jnp.sqrt(jnp.abs(x) * CODE_SCALE))
    return jnp.where(x < 0.0, -root, root)


def decode(code):
    square = code * code
    return jnp.where(code < 0.0, -square, square) * square * (1.0 / CODE_SCALE)


def window_kernel(count, slip_hbm, ids_hbm, table_hbm, out, slip, ids, table, sems):
    q = lax.axis_index("freq")
    copies = [
        pltpu.make_async_copy(table_hbm.at[q], table, sems.at[0]),
        pltpu.make_async_copy(slip_hbm, slip, sems.at[1]),
        pltpu.make_async_copy(ids_hbm, ids, sems.at[2]),
    ]
    for copy in copies:
        copy.start()
    out[CAP:ID_ROW, :] = jnp.zeros((ID_ROW - CAP, 128), f32)
    out[ID_ROW:HOLD, :] = jnp.full((HOLD - ID_ROW, 128), -1.0, f32)
    copies[0].wait()
    both = jnp.concatenate(split2(table[...]), axis=1)
    copies[1].wait()
    r = jnp.dot(slip[...], both, preferred_element_type=f32)
    out[0:CAP, :] = encode(r[:, :128] + r[:, 128:])
    copies[2].wait()
    live = lanes((1, CAP)) < count[0]
    out[ID_ROW : ID_ROW + 1, 0:CAP] = jnp.where(live, ids[...].astype(f32), -1.0)


def route_kernel(held, out):
    core = lax.rem(lax.axis_index("patch"), 2).astype(f32)
    n = 16 * 24
    r = rows((n, 128))
    d = lax.shift_right_logical(r * 2731, 16)
    j = lax.shift_right_logical(r - 24 * d, 1)
    base = (96 * d + 4 * j).astype(f32)
    base = base + 48.0 * core
    block = lax.shift_right_logical(lanes((HOLD, 256)), 5) % 4
    odd = lax.rem(lax.shift_right_logical(lanes((HOLD, 128)), 5), 2) == 1
    pad = jnp.zeros((128 - HOLD, 256), f32)
    left, right_hi, right_lo = [], [], []
    for k in range(2):
        x = held[k]
        re = jnp.where(odd, pltpu.roll(x, 32, 1), x)
        im = jnp.where(odd, x, pltpu.roll(x, 96, 1))
        hi, lo = split2(jnp.concatenate([re, im], axis=1))
        hi, lo = hi.astype(f32), lo.astype(f32)
        ahead = held[k, ID_ROW : ID_ROW + 1, :] - base
        for b in range(4):
            left.append(jnp.where(ahead == float(b), 1.0, 0.0))
            right_hi += [jnp.where(block == b, hi, 0.0), pad]
            right_lo += [jnp.where(block == b, lo, 0.0), pad]
    lhs = jnp.concatenate(left, axis=1).astype(bf16)
    rhs_hi = jnp.concatenate(right_hi, axis=0).astype(bf16)
    rhs_lo = jnp.concatenate(right_lo, axis=0).astype(bf16)
    got = jnp.dot(lhs, rhs_hi, preferred_element_type=f32) + jnp.dot(
        lhs, rhs_lo, preferred_element_type=f32
    )
    even = lax.rem(r, 2) == 0
    out[...] = jnp.where(even, got[:, :128], got[:, 128:]).reshape(16, 24, 128)


def sublane_sums(parts):
    sub = rows((8, 128))
    dist = 4
    while dist >= 1:
        low = (lax.shift_right_logical(sub, dist.bit_length() - 1) % 2) == 0
        parts = [
            jnp.where(low, a, b) + pltpu.roll(jnp.where(low, b, a), dist, 0)
            if dist == 4
            else jnp.where(low, a, b)
            + jnp.where(
                low, pltpu.roll(a, 8 - dist, 0), pltpu.roll(b, dist, 0)
            )
            for a, b in zip(parts[: len(parts) // 2], parts[len(parts) // 2 :])
        ]
        dist //= 2
    return parts[0]


def moment_kernel(green, moments, out, weights):
    spread = jnp.where(
        rows((OWN, OWN * BINS)) == lax.shift_right_logical(lanes((OWN, OWN * BINS)), 5),
        1.0,
        0.0,
    ).astype(bf16)
    hi, lo = split2(moments[...])
    w = jnp.dot(hi, spread, preferred_element_type=f32) + jnp.dot(
        lo, spread, preferred_element_type=f32
    )
    for m in range(6):
        weights[m] = jnp.broadcast_to(w[m : m + 1], (2, OWN * BINS))
    n_rows = 3 * STA_DEV
    for i in range(0, n_rows, 8):
        n = min(8, n_rows - i)
        acc = None
        for m in range(6):
            at = m * n_rows + i
            term = green[at : at + n].astype(f32) * weights[m][None]
            acc = term if acc is None else acc + term
        for j in range(12):
            out[i : i + n, 2 * j : 2 * j + 2, :] = acc[:, :, 128 * j : 128 * j + 128]


def patch_kernel(tiles, got, out):
    s = got[...]
    even = lax.rem(rows((24, 128)), 2) == 0
    for_re = jnp.where(even, s, -s)
    for_im = jnp.where(even, pltpu.roll(s, 23, 0), pltpu.roll(s, 1, 0))
    lane = lanes((8, 128))
    half = lane < 64
    block_even = lax.rem(lax.shift_right_logical(lane, 5), 2) == 0
    folded = []
    for c in range(3):
        for s0 in range(0, 32, 8):
            n = min(8, STA_DEV - s0)
            at = c * STA_DEV + s0
            acc = tiles[at : at + n]
            sums = []
            for weight in (for_re, for_im):
                p = (acc * weight[None]).reshape(n, 3, 8, 128)
                p = p[:, 0] + p[:, 1] + p[:, 2]
                parts = [p[i] for i in range(n)] + [jnp.zeros((8, 128), f32)] * (8 - n)
                sums.append(sublane_sums(parts))
            a, b = sums
            folded.append(
                jnp.where(half, a, b) + pltpu.roll(jnp.where(half, b, a), 64, 1)
            )
    for i in range(6):
        a, b = folded[i], folded[i + 6]
        w = jnp.where(block_even, a, b)
        z = jnp.where(block_even, pltpu.roll(a, 96, 1), pltpu.roll(b, 32, 1))
        out[8 * i : 8 * i + 8, :] = w + z


def spread_half_kernel(got, out):
    total = jnp.sum(got[...], axis=0).astype(bf16)
    out[...] = jnp.broadcast_to(total[None], out.shape)


def series_kernel(turn, got, table, out):
    p = lax.axis_index("patch")
    x = jnp.sum(got[...].astype(f32), axis=0)
    other = pltpu.roll(x, 64, 1)
    real = lanes((48, 128)) < 64
    turned = turn[p]
    x = turned[0:1] * x + turned[1:2] * jnp.where(real, -other, other)
    hi, lo = split2(x)
    lhs = jnp.concatenate([hi, lo, hi], axis=1)
    t_hi, t_lo = split2(table[...])
    rhs = jnp.concatenate([t_hi, t_hi, t_lo], axis=0)
    y = jnp.dot(lhs, rhs, preferred_element_type=f32)
    y = jnp.concatenate([y[:, :128], y[:, 128:]], axis=0)
    for c in range(3):
        out[c] = y[32 * c : 32 * c + STA_DEV]


VMEM = pl.BlockSpec(memory_space=pltpu.VMEM)
SMEM = pl.BlockSpec(memory_space=pltpu.SMEM)


HBM = pl.BlockSpec(memory_space=pltpu.HBM)


def call(kernel, shape, specs, *args, dtype=f32, scratch=(), grant=32):
    return pl.pallas_call(
        kernel,
        out_shape=jax.ShapeDtypeStruct(shape, dtype),
        in_specs=specs,
        out_specs=VMEM,
        scratch_shapes=scratch,
        compiler_params=pltpu.CompilerParams(vmem_limit_bytes=grant * 1024 * 1024),
    )(*args)


def local(slip_rate, face_counts, patch_ids, moments, green):
    held = call(
        window_kernel,
        (HOLD, 128),
        [SMEM] + [HBM] * 3,
        face_counts,
        slip_rate,
        patch_ids.reshape(1, CAP),
        jnp.asarray(analysis_table()),
        scratch=[
            pltpu.VMEM((CAP, T // WINDOWS), bf16),
            pltpu.VMEM((1, CAP), jnp.int32),
            pltpu.VMEM((T // WINDOWS, 128), f32),
            pltpu.SemaphoreType.DMA((3,)),
        ],
        grant=60,
    )
    held = lax.all_gather(held, "patch", axis_index_groups=CORE_PAIRS)
    blocks = call(route_kernel, (16, 24, 128), [VMEM], held).astype(f16)
    blocks = lax.all_to_all(
        blocks, "patch", 0, 0, axis_index_groups=SAME_CORE, tiled=True
    )
    green = green.transpose(0, 2, 3, 1, 4).reshape(6 * 3 * STA_DEV, 2, OWN * BINS)
    tiles = call(
        moment_kernel,
        (3 * STA_DEV, 24, 128),
        [VMEM, VMEM],
        green,
        moments.T,
        scratch=[pltpu.VMEM((6, 2, OWN * BINS), f32)],
    )
    code = jnp.sum(blocks.astype(f32), axis=0).astype(f16)
    code, tiles = lax.optimization_barrier((code, tiles))
    codes = jnp.broadcast_to(code[None], (WINDOWS, 24, 128))
    codes = lax.all_to_all(
        codes, "freq", 0, 0, axis_index_groups=WINDOW_GROUP, tiled=True
    )
    spectra = jnp.sum(decode(codes.astype(f32)), axis=0)
    partial = call(patch_kernel, (48, 128), [VMEM, VMEM], tiles, spectra)
    pair = lax.all_gather(partial, "patch", axis_index_groups=CORE_PAIRS)
    copies = call(spread_half_kernel, (16, 48, 128), [VMEM], pair, dtype=bf16)
    copies = lax.all_to_all(
        copies, "patch", 0, 0, axis_index_groups=SAME_CORE, tiled=True
    )
    return call(
        series_kernel,
        (3, STA_DEV, 128),
        [VMEM, VMEM, VMEM],
        jnp.asarray(turns(FACES)),
        copies,
        jnp.asarray(synthesis_table()),
    )


def solution(mesh):
    return jax.shard_map(
        local,
        mesh=mesh,
        in_specs=(
            P("patch", "freq"),
            P("patch"),
            P("patch"),
            P("patch", None),
            P(None, None, None, "freq", "patch"),
        ),
        out_specs=P(None, "freq", "patch"),
        check_vma=False,
    )
```

```python
import functools
import math

import jax
import jax.numpy as jnp
import numpy as np
from jax import lax
from jax.experimental import pallas as pl
from jax.experimental.pallas import tpu as pltpu
from jax.sharding import PartitionSpec as P

T = 4096
BINS = 32
FACES = 32
WINDOWS = 16
CAP = 84
OWN = 48
STA_DEV = 31
HOLD = 96
ID_ROW = 88

CORE_PAIRS = [[2 * d, 2 * d + 1] for d in range(16)]
FROM_TOP = [
    [16 * x + 2 * ((z + 7) % 8) + c for x in range(2) for z in range(8)] for c in range(2)
]
SAME_CORE = [[2 * d + c for d in range(16)] for c in range(2)]
DOWN_Y = [4, 3, 2, 1, 0, 7, 6, 5]
WINDOW_GROUP = [[2 * y + x for x in (1, 0) for y in DOWN_Y]]

CODE_SCALE = 2.0**56

f32 = jnp.float32
bf16 = jnp.bfloat16
f16 = jnp.float16


def split2(x):
    hi = x.astype(bf16)
    return hi, (x - hi.astype(f32)).astype(bf16)


def angles(samples):
    k = 1 + np.arange(BINS) * (T // (2 * BINS))
    return 2.0 * np.pi * ((np.arange(samples)[:, None] * k[None, :]) % T) / T


def analysis_table():
    t = np.arange(T)[:, None]
    k = 1 + np.arange(BINS) * (T // (2 * BINS))
    ang = 2.0 * np.pi * ((t * k) % T) / T
    c, s = np.cos(ang) / math.sqrt(T), -np.sin(ang) / math.sqrt(T)
    table = np.concatenate([c, s, c, s], axis=1).astype(np.float32)
    return table.reshape(WINDOWS, T // WINDOWS, 128)


def synthesis_table():
    ang = angles(T // FACES).T
    c, s = np.cos(ang) / math.sqrt(BINS), -np.sin(ang) / math.sqrt(BINS)
    z = np.zeros_like(c)
    first = np.concatenate([c, z, s, z], axis=0)
    second = np.concatenate([z, c, z, s], axis=0)
    return np.concatenate([first, second], axis=1).astype(np.float32)


def turns(n):
    a = 2.0 * np.pi * np.arange(n) / n
    both = np.stack([np.cos(a), np.sin(a)], axis=1).astype(np.float32)
    return np.broadcast_to(both[:, :, None], (n, 2, 128)).copy()


def lanes(shape):
    return lax.broadcasted_iota(jnp.int32, shape, len(shape) - 1)


def rows(shape):
    return lax.broadcasted_iota(jnp.int32, shape, len(shape) - 2)


def encode(x):
    root = jnp.sqrt(jnp.sqrt(jnp.abs(x) * CODE_SCALE))
    return jnp.where(x < 0.0, -root, root)


def decode(code):
    square = code * code
    return jnp.where(code < 0.0, -square, square) * square * (1.0 / CODE_SCALE)


def window_kernel(count_hbm, slip_hbm, ids_hbm, table_hbm, out, count, slip, ids, table, sems):
    q = lax.axis_index("freq")
    copies = [
        pltpu.make_async_copy(table_hbm.at[q], table, sems.at[0]),
        pltpu.make_async_copy(slip_hbm, slip, sems.at[1]),
        pltpu.make_async_copy(ids_hbm, ids, sems.at[2]),
        pltpu.make_async_copy(count_hbm, count, sems.at[3]),
    ]
    for copy in copies:
        copy.start()
    out[CAP:ID_ROW, :] = jnp.zeros((ID_ROW - CAP, 128), f32)
    out[ID_ROW:HOLD, :] = jnp.full((HOLD - ID_ROW, 128), -1.0, f32)
    for copy in copies:
        copy.wait()
    both = jnp.concatenate(split2(table[...]), axis=1)
    r = jnp.dot(slip[...], both, preferred_element_type=f32)
    out[0:CAP, :] = encode(r[:, :128] + r[:, 128:])
    live = lanes((1, CAP)) < count[...]
    out[ID_ROW : ID_ROW + 1, 0:CAP] = jnp.where(live, ids[...].astype(f32), -1.0)


def route_kernel(held, out):
    core = lax.rem(lax.axis_index("patch"), 2).astype(f32)
    n = 16 * 24
    r = rows((n, 128))
    d = lax.shift_right_logical(r * 2731, 16)
    j = lax.shift_right_logical(r - 24 * d, 1)
    place = 8 * lax.shift_right_logical(d, 3) + ((d + 7) & 7)
    base = (96 * place + 4 * j).astype(f32)
    base = base + 48.0 * core
    block = lax.shift_right_logical(lanes((HOLD, 256)), 5) % 4
    odd = lax.rem(lax.shift_right_logical(lanes((HOLD, 128)), 5), 2) == 1
    pad = jnp.zeros((128 - HOLD, 256), f32)
    left, right_hi, right_lo = [], [], []
    for k in range(2):
        x = held[k]
        re = jnp.where(odd, pltpu.roll(x, 32, 1), x)
        im = jnp.where(odd, x, pltpu.roll(x, 96, 1))
        hi, lo = split2(jnp.concatenate([re, im], axis=1))
        hi, lo = hi.astype(f32), lo.astype(f32)
        ahead = held[k, ID_ROW : ID_ROW + 1, :] - base
        for b in range(4):
            left.append(jnp.where(ahead == float(b), 1.0, 0.0))
            right_hi += [jnp.where(block == b, hi, 0.0), pad]
            right_lo += [jnp.where(block == b, lo, 0.0), pad]
    lhs = jnp.concatenate(left, axis=1).astype(bf16)
    rhs_hi = jnp.concatenate(right_hi, axis=0).astype(bf16)
    rhs_lo = jnp.concatenate(right_lo, axis=0).astype(bf16)
    got = jnp.dot(lhs, rhs_hi, preferred_element_type=f32) + jnp.dot(
        lhs, rhs_lo, preferred_element_type=f32
    )
    even = lax.rem(r, 2) == 0
    out[...] = jnp.where(even, got[:, :128], got[:, 128:]).reshape(16, 24, 128)


def sublane_sums(parts):
    sub = rows((8, 128))
    dist = 4
    while dist >= 1:
        low = (lax.shift_right_logical(sub, dist.bit_length() - 1) % 2) == 0
        parts = [
            jnp.where(low, a, b) + pltpu.roll(jnp.where(low, b, a), dist, 0)
            if dist == 4
            else jnp.where(low, a, b)
            + jnp.where(
                low, pltpu.roll(a, 8 - dist, 0), pltpu.roll(b, dist, 0)
            )
            for a, b in zip(parts[: len(parts) // 2], parts[len(parts) // 2 :])
        ]
        dist //= 2
    return parts[0]


def moment_kernel(green, moments, out, weights):
    spread = jnp.where(
        rows((OWN, OWN * BINS)) == lax.shift_right_logical(lanes((OWN, OWN * BINS)), 5),
        1.0,
        0.0,
    ).astype(bf16)
    hi, lo = split2(moments[...])
    w = jnp.dot(hi, spread, preferred_element_type=f32) + jnp.dot(
        lo, spread, preferred_element_type=f32
    )
    for m in range(6):
        weights[m] = jnp.broadcast_to(w[m : m + 1], (2, OWN * BINS))
    n_rows = 3 * STA_DEV
    for i in range(0, n_rows, 8):
        n = min(8, n_rows - i)
        acc = None
        for m in range(6):
            at = m * n_rows + i
            term = green[at : at + n].astype(f32) * weights[m][None]
            acc = term if acc is None else acc + term
        for j in range(12):
            out[i : i + n, 2 * j : 2 * j + 2, :] = acc[:, :, 128 * j : 128 * j + 128]


def patch_kernel(tiles, got, out):
    s = got[...]
    even = lax.rem(rows((24, 128)), 2) == 0
    for_re = jnp.where(even, s, -s)
    for_im = jnp.where(even, pltpu.roll(s, 23, 0), pltpu.roll(s, 1, 0))
    lane = lanes((8, 128))
    half = lane < 64
    block_even = lax.rem(lax.shift_right_logical(lane, 5), 2) == 0
    folded = []
    for c in range(3):
        for s0 in range(0, 32, 8):
            n = min(8, STA_DEV - s0)
            at = c * STA_DEV + s0
            acc = tiles[at : at + n]
            sums = []
            for weight in (for_re, for_im):
                p = (acc * weight[None]).reshape(n, 3, 8, 128)
                p = p[:, 0] + p[:, 1] + p[:, 2]
                parts = [p[i] for i in range(n)] + [jnp.zeros((8, 128), f32)] * (8 - n)
                sums.append(sublane_sums(parts))
            a, b = sums
            folded.append(
                jnp.where(half, a, b) + pltpu.roll(jnp.where(half, b, a), 64, 1)
            )
    for i in range(6):
        a, b = folded[i], folded[i + 6]
        w = jnp.where(block_even, a, b)
        z = jnp.where(block_even, pltpu.roll(a, 96, 1), pltpu.roll(b, 32, 1))
        out[8 * i : 8 * i + 8, :] = w + z


def spread_half_kernel(got, out):
    total = jnp.sum(got[...], axis=0).astype(bf16)
    out[...] = jnp.broadcast_to(total[None], out.shape)


def series_kernel(turn, got, table, out):
    p = lax.axis_index("patch")
    x = jnp.sum(got[...].astype(f32), axis=0)
    other = pltpu.roll(x, 64, 1)
    real = lanes((48, 128)) < 64
    turned = turn[p]
    x = turned[0:1] * x + turned[1:2] * jnp.where(real, -other, other)
    hi, lo = split2(x)
    lhs = jnp.concatenate([hi, lo, hi], axis=1)
    t_hi, t_lo = split2(table[...])
    rhs = jnp.concatenate([t_hi, t_hi, t_lo], axis=0)
    y = jnp.dot(lhs, rhs, preferred_element_type=f32)
    y = jnp.concatenate([y[:, :128], y[:, 128:]], axis=0)
    for c in range(3):
        out[c] = y[32 * c : 32 * c + STA_DEV]


VMEM = pl.BlockSpec(memory_space=pltpu.VMEM)
SMEM = pl.BlockSpec(memory_space=pltpu.SMEM)


HBM = pl.BlockSpec(memory_space=pltpu.HBM)


def call(kernel, shape, specs, *args, dtype=f32, scratch=(), grant=32):
    return pl.pallas_call(
        kernel,
        out_shape=jax.ShapeDtypeStruct(shape, dtype),
        in_specs=specs,
        out_specs=VMEM,
        scratch_shapes=scratch,
        compiler_params=pltpu.CompilerParams(vmem_limit_bytes=grant * 1024 * 1024),
    )(*args)


def local(slip_rate, face_counts, patch_ids, moments, green):
    held = call(
        window_kernel,
        (HOLD, 128),
        [HBM] * 4,
        face_counts.reshape(1, 1),
        slip_rate,
        patch_ids.reshape(1, CAP),
        jnp.asarray(analysis_table()),
        scratch=[
            pltpu.VMEM((1, 1), jnp.int32),
            pltpu.VMEM((CAP, T // WINDOWS), bf16),
            pltpu.VMEM((1, CAP), jnp.int32),
            pltpu.VMEM((T // WINDOWS, 128), f32),
            pltpu.SemaphoreType.DMA((4,)),
        ],
        grant=60,
    )
    held = lax.all_gather(held, "patch", axis_index_groups=CORE_PAIRS)
    blocks = call(route_kernel, (16, 24, 128), [VMEM], held).astype(f16)
    blocks = lax.all_to_all(
        blocks, "patch", 0, 0, axis_index_groups=FROM_TOP, tiled=True
    )
    green = green.transpose(0, 2, 3, 1, 4).reshape(6 * 3 * STA_DEV, 2, OWN * BINS)
    tiles = call(
        moment_kernel,
        (3 * STA_DEV, 24, 128),
        [VMEM, VMEM],
        green,
        moments.T,
        scratch=[pltpu.VMEM((6, 2, OWN * BINS), f32)],
    )
    code = jnp.sum(blocks.astype(f32), axis=0).astype(f16)
    code, tiles = lax.optimization_barrier((code, tiles))
    codes = jnp.broadcast_to(code[None], (WINDOWS, 24, 128))
    codes = lax.all_to_all(
        codes, "freq", 0, 0, axis_index_groups=WINDOW_GROUP, tiled=True
    )
    spectra = jnp.sum(decode(codes.astype(f32)), axis=0)
    partial = call(patch_kernel, (48, 128), [VMEM, VMEM], tiles, spectra)
    pair = lax.all_gather(partial, "patch", axis_index_groups=CORE_PAIRS)
    copies = call(spread_half_kernel, (16, 48, 128), [VMEM], pair, dtype=bf16)
    copies = lax.all_to_all(
        copies, "patch", 0, 0, axis_index_groups=SAME_CORE, tiled=True
    )
    return call(
        series_kernel,
        (3, STA_DEV, 128),
        [VMEM, VMEM, VMEM],
        jnp.asarray(turns(FACES)),
        copies,
        jnp.asarray(synthesis_table()),
    )


def solution(mesh):
    return jax.shard_map(
        local,
        mesh=mesh,
        in_specs=(
            P("patch", "freq"),
            P("patch"),
            P("patch"),
            P("patch", None),
            P(None, None, None, "freq", "patch"),
        ),
        out_specs=P(None, "freq", "patch"),
        check_vma=False,
    )
```
